1024 devices in a mesh: coarse: 16 (over x, z_hi, core), sub: 64 (over z_lo, y).
Axes of the slice: x: 4, y: 8, z: 16 (z_hi: 2, z_lo: 8; z = z_hi * 8 + z_lo), core: 2. Of those that a mesh axis runs over, the one named last changes fastest.
Arguments:
- face_loads: float32 [16, 64, 6, 64, 128], P('coarse', 'sub'), may hold values from -18 to 18
- schur_blocks: float32 [16, 64, 384, 384], P('coarse', 'sub'), may hold values from -8 to 70, as said below
- coarse_basis: float32 [16, 64, 384, 32], P('coarse', 'sub'), may hold values from -0.75 to 0.75
- drop_masks: int32 [16, 64, 6, 64], P('coarse', 'sub'), may hold values 0 or 1
- coarse_inverse: float32 [64, 512, 512], P('sub', 'coarse'), may hold values from -1 to 3, as said below
Outputs:
- solution: float32 [16, 64, 6, 64, 128], P('coarse', 'sub')
- residual: float32 [16, 64, 6, 64, 128], P('coarse', 'sub')
The draws below stay inside these ranges and needn't reach their ends.
Inputs may be any that keep to these rules, and one draw needn't show every extreme that they name: `schur_blocks`: each subdomain's block is symmetric positive definite. `coarse_inverse`: each group's matrix is symmetric positive definite.
All inputs are finite; a program needn't handle non-finite values. No bound on the sum of `drop_masks` on one device may be relied on, other than what follows from the above.
Results may differ from the reference program's by a relative error of at most 0.0003.
Values sent between devices are 32-bit elements; how exact they have to be, the bound alone decides.
A program may use at most 32 MiB of HBM per device.

```python
import math
import jax
import jax.numpy as jnp
from jax import lax

FACES = 6
FACE_DOFS = 64
CASES = 128
COARSE_DOFS = 32
ROW = 8
ITERS = 2
COARSE_BLOCKS = 16
SUB_BLOCKS = 64
GROUP_DOFS = 512


def symmetric_dominant(key, extent, lowest, topmost):
    first_key, second_key = jax.random.split(key)
    uniform_part = jax.random.uniform(first_key, (extent, extent), jnp.float32, -1.0, 1.0)
    paired = (uniform_part + uniform_part.T) * (1.0 / math.sqrt(extent))
    scales = jnp.exp(jax.random.uniform(second_key, (extent,), jnp.float32, math.log(lowest), math.log(topmost)))
    dominant = paired + 3.5 * jnp.eye(extent, dtype=jnp.float32)
    return scales[:, None] * dominant * scales[None, :]


def draw_schur_blocks(key, part):
    key = jax.random.fold_in(key, 11)
    lowest, topmost = (1.0, 3.0)
    extent = FACES * FACE_DOFS
    keys = jax.random.split(key, COARSE_BLOCKS * SUB_BLOCKS)
    blocks = lax.map(lambda single: symmetric_dominant(single, extent, lowest, topmost), keys)
    return blocks.reshape(COARSE_BLOCKS, SUB_BLOCKS, extent, extent)


def draw_coarse_inverse(key, part):
    key = jax.random.fold_in(key, 23)
    lowest, topmost = (0.3, 0.6)
    keys = jax.random.split(key, SUB_BLOCKS)
    return lax.map(lambda single: symmetric_dominant(single, GROUP_DOFS, lowest, topmost), keys)


def draw_face_loads(key, part):
    key = jax.random.fold_in(key, 37)
    first_key = jax.random.fold_in(key, 0)
    domains = COARSE_BLOCKS * SUB_BLOCKS
    ramp = 1.0 + 2.0 * jnp.arange(domains, dtype=jnp.float32) / max(domains - 1, 1)
    ramp = ramp.reshape(COARSE_BLOCKS, SUB_BLOCKS, 1, 1, 1)
    shape = (COARSE_BLOCKS, SUB_BLOCKS, FACES, FACE_DOFS, CASES)
    values = jnp.clip(jax.random.normal(first_key, shape, jnp.float32), -5.0, 5.0)
    return values * ramp


def plant(entries, stream_key, least, largest):
    longest = entries.shape.index(max(entries.shape))
    spots = []
    for shift in (0, 1):
        where = [jax.random.randint(jax.random.fold_in(stream_key, axis), (), 0, length) for axis, length in enumerate(entries.shape)]
        where[longest] = (where[longest] + shift) % entries.shape[longest]
        spots.append(tuple(where))
    return entries.at[spots[0]].set(least).at[spots[1]].set(largest)


def level_of(own_key, shape, pieces, low, top_value):
    gain, own = 1.0, jax.random.fold_in(own_key, 6)
    for position, blocks in pieces:
        steps = jnp.exp(jax.random.uniform(jax.random.fold_in(own, position), (blocks,), jnp.float32, low / len(pieces), top_value / len(pieces)))
        gain = gain * jnp.repeat(steps, shape[position] // blocks).reshape([-1 if axis == position else 1 for axis in range(len(shape))])
    return gain


def scatter_about(stream_key, shape, width, reach, shards=(), kind=jnp.bfloat16):
    entries = jax.random.normal(stream_key, shape, jnp.float32) * width
    if len(shards) > 0:
        entries = level_of(stream_key, shape, shards, -0.22, 0.18) * entries
    return jnp.clip(entries, min=-reach, max=reach).astype(kind)


def setup_inputs(seed: int = 0) -> dict:
    seeds = jax.random.split(jax.random.key(seed), 6)
    return {
        "face_loads": draw_face_loads(jax.random.fold_in(seeds[5], 71), 0),
        "schur_blocks": draw_schur_blocks(jax.random.fold_in(seeds[5], 71), 0),
        "coarse_basis": scatter_about(seeds[2], (COARSE_BLOCKS, SUB_BLOCKS, FACES * FACE_DOFS, COARSE_DOFS), (2 * COARSE_DOFS) ** -0.5, 0.75, ((0, 16), (1, 64)), jnp.float32),
        "drop_masks": plant((jax.random.randint(seeds[3], (COARSE_BLOCKS, SUB_BLOCKS, FACES, FACE_DOFS), 0, 4) < 1).astype(jnp.int32), jax.random.fold_in(seeds[3], 1), 0, 1),
        "coarse_inverse": draw_coarse_inverse(jax.random.fold_in(seeds[5], 71), 0),
    }


highest = lax.Precision.HIGHEST

def assemble(values):
    coarse_count, sub_count = (values.shape[0], values.shape[1])
    zero_layer = jnp.zeros_like(values[:1, :, 0])
    from_lower = jnp.concatenate([zero_layer, values[:-1, :, 1]], axis=0)
    from_upper = jnp.concatenate([values[1:, :, 0], zero_layer], axis=0)
    zero_single = jnp.zeros_like(values[:, :1, 0])
    row_lower = jnp.concatenate([zero_single, values[:, :-1, 3]], axis=1)
    row_upper = jnp.concatenate([values[:, 1:, 2], zero_single], axis=1)
    zero_rows = jnp.zeros_like(values[:, :ROW, 0])
    column_lower = jnp.concatenate([zero_rows, values[:, :sub_count - ROW, 5]], axis=1)
    column_upper = jnp.concatenate([values[:, ROW:, 4], zero_rows], axis=1)
    incoming = jnp.stack([from_lower, from_upper, row_lower, row_upper, column_lower, column_upper], axis=2)
    return values + incoming

def local_solve(packed):
    schur_one, scale_one, basis_one, rhs_one = packed
    operator = scale_one * schur_one * scale_one.reshape(1, -1)
    factor = jnp.linalg.cholesky(operator + jnp.dot(basis_one.astype(jnp.float32), basis_one.T.astype(jnp.float32), precision=highest, preferred_element_type=jnp.float32))
    return jax.scipy.linalg.cho_solve((factor, True), rhs_one)

def reference(face_loads, schur_blocks, coarse_basis, drop_masks, coarse_inverse):
    coarse_count, sub_count, face_count, dof_count, case_count = face_loads.shape
    order_size = face_count * dof_count
    domains = coarse_count * sub_count
    basis_width = coarse_basis.shape[3]
    coarse_at = jnp.broadcast_to(jnp.arange(coarse_count).reshape(-1, 1), (coarse_count, sub_count))
    sub_at = jnp.broadcast_to(jnp.arange(sub_count).reshape(1, -1), (coarse_count, sub_count))
    present = jnp.stack([coarse_at > 0, coarse_at < coarse_count - 1, sub_at > 0, sub_at < sub_count - 1, sub_at >= ROW, sub_at < sub_count - ROW], axis=2)
    weights = jnp.where(present, 0.5, 1.0).astype(jnp.float32)[:, :, :, None, None]
    scaling = (1.0 + drop_masks.astype(jnp.float32)).reshape(domains, order_size, 1)
    schur_flat = schur_blocks.reshape(domains, order_size, order_size)
    basis_flat = coarse_basis.reshape(domains, order_size, basis_width)

    def apply_operator(vector):
        flat = vector.reshape(domains, order_size, case_count)
        mapped = scaling * jnp.einsum('dij,djr->dir', schur_flat, scaling * flat, precision=highest)
        return mapped.reshape(coarse_count, sub_count, face_count, dof_count, case_count)

    def precondition(vector):
        weighted = (weights * vector).reshape(domains, order_size, case_count)
        restricted = jnp.einsum('dik,dir->dkr', basis_flat, weighted, precision=highest)
        grouped = restricted.reshape(coarse_count, sub_count, basis_width, case_count).transpose(1, 0, 2, 3).reshape(sub_count, coarse_count * basis_width, case_count)
        solved = jnp.einsum('sij,sjr->sir', coarse_inverse, grouped, precision=highest)
        coarse_part = solved.reshape(sub_count, coarse_count, basis_width, case_count).transpose(1, 0, 2, 3).reshape(domains, basis_width, case_count)
        local_part = lax.map(local_solve, (schur_flat, scaling, basis_flat, weighted))
        combined = local_part + jnp.einsum('dik,dkr->dir', basis_flat, coarse_part, precision=highest)
        return assemble(weights * combined.reshape(coarse_count, sub_count, face_count, dof_count, case_count))

    def inner(former, latter):
        return jnp.sum(weights * former * latter, axis=(0, 1, 2, 3))
    residual = assemble(face_loads)
    solution = jnp.zeros_like(residual)
    precond = precondition(residual)
    direction = precond
    gamma_now = inner(residual, precond)
    for sweep_index in range(ITERS):
        mapped = assemble(apply_operator(direction))
        step_size = gamma_now / inner(direction, mapped)
        solution = solution + step_size * direction
        residual = residual - step_size * mapped
        if sweep_index + 1 < ITERS:
            precond = precondition(residual)
            gamma_next = inner(residual, precond)
            direction = precond + gamma_next / gamma_now * direction
            gamma_now = gamma_next
    return (solution, residual)
```

```python
import jax
import jax.numpy as jnp
from jax import lax
from jax.experimental import pallas as pl
from jax.experimental.pallas import tpu as pltpu
from jax.sharding import PartitionSpec as P

ROW = 8
X_COUNT, HALF_COUNT, CORE_COUNT = 4, 2, 2
LOW_COUNT, Y_COUNT = 8, 8
LEAF = 128
GROUP = 8

MESH = pl.DeviceIdType.MESH
highest = lax.Precision.HIGHEST


def dot(former, latter):
    return jnp.dot(former, latter, precision=highest, preferred_element_type=jnp.float32)


def dot_left_transposed(former, latter):
    return lax.dot_general(
        former, latter, (((0,), (0,)), ((), ())), precision=highest, preferred_element_type=jnp.float32
    )


def dot_right_transposed(former, latter):
    return lax.dot_general(
        former, latter, (((1,), (1,)), ((), ())), precision=highest, preferred_element_type=jnp.float32
    )


def reciprocal(value):
    guess = pl.reciprocal(value, approx=True)
    guess = guess * (2.0 - value * guess)
    return guess * (2.0 - value * guess)


def product(former, latter):
    out = []
    for row in former:
        line = []
        for j in range(len(latter[0])):
            total = row[0] * latter[0][j]
            for t in range(1, len(latter)):
                total = total + row[t] * latter[t][j]
            line.append(total)
        out.append(line)
    return out


def small_inverse(matrix):
    size = len(matrix)
    if size == 2:
        a, b, c = matrix[0][0], matrix[0][1], matrix[1][1]
        det = reciprocal(a * c - b * b)
        return [[c * det, -b * det], [-b * det, a * det]]
    half = size // 2
    corner = [row[half:] for row in matrix[:half]]
    first = small_inverse([row[:half] for row in matrix[:half]])
    carried = product(first, corner)
    rest = [[None] * half for _ in range(half)]
    for i in range(half):
        for j in range(i, half):
            total = matrix[half + i][half + j]
            for t in range(half):
                total = total - corner[t][i] * carried[t][j]
            rest[i][j] = rest[j][i] = total
    second = small_inverse(rest)
    side = product(carried, second)
    out = [[None] * size for _ in range(size)]
    for i in range(half):
        for j in range(i, half):
            total = first[i][j]
            for t in range(half):
                total = total + side[i][t] * carried[j][t]
            out[i][j] = out[j][i] = total
        for j in range(half):
            out[i][half + j] = out[half + j][i] = -side[i][j]
            out[half + i][half + j] = second[i][j]
    return out


def invert_leaf(leaf_ref):
    shape = (GROUP, LEAF)
    lane = lax.broadcasted_iota(jnp.int32, shape, 1)
    sublane = lax.broadcasted_iota(jnp.int32, shape, 0)

    def step(g, carry):
        base = pl.multiple_of(g * GROUP, GROUP)
        rows = [jnp.broadcast_to(leaf_ref[pl.ds(base + t, 1), :], shape) for t in range(GROUP)]
        pivots = [[None] * GROUP for _ in range(GROUP)]
        for r in range(GROUP):
            for s in range(r, GROUP):
                pivots[r][s] = pivots[s][r] = jnp.broadcast_to(rows[r][:, s : s + 1], shape)
        inverse = small_inverse(pivots)
        unit = [jnp.where(lane == t, 1.0, jnp.where(lane < GROUP, 0.0, rows[t])) for t in range(GROUP)]
        solved = []
        for s in range(GROUP):
            total = inverse[s][0] * unit[0]
            for t in range(1, GROUP):
                total = total + inverse[s][t] * unit[t]
            solved.append(total)
        tile = solved[0]
        for s in range(1, GROUP):
            tile = jnp.where(sublane == s, solved[s], tile)
        for i in range(LEAF // GROUP):
            place = slice(i * GROUP, (i + 1) * GROUP)
            old = leaf_ref[place, :]
            new = jnp.where(lane < GROUP, 0.0, old)
            for s in range(GROUP):
                new = new - jnp.broadcast_to(old[:, s : s + 1], shape) * solved[s]
            leaf_ref[place, :] = pltpu.roll(jnp.where(g == i, tile, new), LEAF - GROUP, 1)
        return carry

    lax.fori_loop(0, LEAF // GROUP, step, 0)


def invert_in_place(matrix_ref, leaf_ref):
    blocks = matrix_ref.shape[0] // LEAF
    for j in range(blocks):
        here = slice(j * LEAF, (j + 1) * LEAF)
        leaf_ref[...] = matrix_ref[here, here]
        invert_leaf(leaf_ref)
        inverse = leaf_ref[...]
        matrix_ref[here, here] = inverse
        others = [slice(i * LEAF, (i + 1) * LEAF) for i in range(blocks) if i != j]
        for columns in others:
            matrix_ref[here, columns] = dot(inverse, matrix_ref[here, columns])
        for rows in others:
            column = matrix_ref[rows, here]
            for columns in others:
                matrix_ref[rows, columns] = matrix_ref[rows, columns] - dot(column, matrix_ref[here, columns])
            matrix_ref[rows, here] = -dot(column, inverse)


def factor_kernel(schur_ref, basis_ref, scaling_column_ref, scaling_row_ref, operator_ref, inverse_ref, leaf_ref):
    operator = scaling_column_ref[...] * schur_ref[...] * scaling_row_ref[...]
    operator_ref[...] = operator
    basis = basis_ref[...]
    inverse_ref[...] = operator + dot_right_transposed(basis, basis)
    invert_in_place(inverse_ref, leaf_ref)


def make_iterate_kernel(sizes):
    x_count, half_count, core_count, low_count, y_count, row_step = sizes
    coarse_count = x_count * half_count * core_count
    sub_count = low_count * y_count
    near_count = x_count * core_count
    far_count = low_count * half_count

    def kernel(
        loads_ref, operator_ref, inverse_ref, basis_ref, rows_ref, solution_ref, residual_ref,
        halo, unsummed, gathered, partner_rows, part, part_in, sums_a, sums_b, sums_c,
        halo_send, halo_recv, near_send, near_recv, pair_send, pair_recv,
        a_send, a_recv, b_send, b_recv, c_send, c_recv,
    ):
        faces, dofs, cases = loads_ref.shape
        order = faces * dofs
        width = basis_ref.shape[1]
        coarse = lax.axis_index("coarse")
        sub = lax.axis_index("sub")
        core = coarse % core_count
        half = (coarse // core_count) % half_count
        x = coarse // (core_count * half_count)
        y = sub % y_count
        low = sub // y_count
        near = x * core_count + core
        far = low * half_count + half

        def near_device(index):
            return ((index // core_count * half_count + half) * core_count + index % core_count, sub)

        def y_device(index):
            return (coarse, low * y_count + index)

        def far_device(index):
            return ((x * half_count + index % half_count) * core_count + core, index // half_count * y_count + y)

        partner = ((x * half_count + (half_count - 1 - half)) * core_count + core, sub)
        present = [
            coarse > 0,
            coarse < coarse_count - 1,
            sub > 0,
            sub < sub_count - 1,
            sub >= row_step,
            sub < sub_count - row_step,
        ]
        neighbour = [
            (coarse - 1, sub),
            (coarse + 1, sub),
            (coarse, sub - 1),
            (coarse, sub + 1),
            (coarse, sub - row_step),
            (coarse, sub + row_step),
        ]

        barrier = pltpu.get_barrier_semaphore()

        def greet(device):
            pl.semaphore_signal(barrier, inc=1, device_id=device, device_id_type=MESH)

        lax.fori_loop(1, near_count, lambda j, c: (greet(near_device((near + j) % near_count)), c)[1], 0)
        lax.fori_loop(1, y_count, lambda j, c: (greet(y_device((y + j) % y_count)), c)[1], 0)
        lax.fori_loop(1, far_count, lambda j, c: (greet(far_device((far + j) % far_count)), c)[1], 0)
        expected = near_count + y_count + far_count - 3
        for face in range(faces):
            expected = expected + present[face].astype(jnp.int32)

            @pl.when(present[face])
            def _():
                greet(neighbour[face])

        weights = [jnp.where(present[face], 0.5, 1.0) for face in range(faces)]
        for face in range(faces):

            @pl.when(jnp.logical_not(present[face]))
            def _():
                for k in range(halo.shape[0]):
                    halo[k, face] = jnp.zeros((dofs, cases), jnp.float32)

        for k in range(gathered.shape[0]):
            for index in range(near_count):
                place = (index // core_count * half_count + (half_count - 1 - half)) * core_count + index % core_count
                gathered[k, place] = jnp.zeros(gathered.shape[2:], jnp.float32)
        pl.semaphore_wait(barrier, expected)

        def halo_copy(k, source, face):
            return pltpu.make_async_remote_copy(
                src_ref=source.at[face],
                dst_ref=halo.at[k, face ^ 1],
                send_sem=halo_send.at[k, face],
                recv_sem=halo_recv.at[k, face ^ 1],
                device_id=neighbour[face],
                device_id_type=MESH,
            )

        def halo_start(k, source):
            for face in range(faces):

                @pl.when(present[face])
                def _():
                    halo_copy(k, source, face).start()

        def halo_wait(k, source):
            for face in range(faces):

                @pl.when(present[face])
                def _():
                    halo_copy(k, source, face ^ 1).wait_recv()

        def halo_finish(k, source):
            for face in range(faces):

                @pl.when(present[face])
                def _():
                    halo_copy(k, source, face).wait_send()

        def pair_copy(k, source, target):
            return pltpu.make_async_remote_copy(
                src_ref=source,
                dst_ref=target,
                send_sem=pair_send.at[k],
                recv_sem=pair_recv.at[k],
                device_id=partner,
                device_id_type=MESH,
            )

        def spread_copy(buffer, send, recv, k, mine, device, slot, index):
            return pltpu.make_async_remote_copy(
                src_ref=buffer.at[k, mine],
                dst_ref=buffer.at[k, slot],
                send_sem=send.at[k, index],
                recv_sem=recv.at[k, slot],
                device_id=device,
                device_id_type=MESH,
            )

        def spread_start(buffer, send, recv, k, mine, count, device_of):
            def body(j, carry):
                index = (mine + j) % count
                spread_copy(buffer, send, recv, k, mine, device_of(index), mine, index).start()
                return carry

            lax.fori_loop(1, count, body, 0)

        def spread_wait(buffer, send, recv, k, mine, count, device_of):
            def body(j, carry):
                index = (mine + j) % count
                spread_copy(buffer, send, recv, k, mine, device_of(index), index, index).wait_recv()
                return carry

            lax.fori_loop(1, count, body, 0)

        def spread_finish(buffer, send, recv, k, mine, count, device_of):
            def body(j, carry):
                index = (mine + j) % count
                spread_copy(buffer, send, recv, k, mine, device_of(index), mine, index).wait_send()
                return carry

            lax.fori_loop(1, count, body, 0)

        stages = [
            (sums_a, a_send, a_recv, near, near_count, near_device),
            (sums_b, b_send, b_recv, y, y_count, y_device),
            (sums_c, c_send, c_recv, far, far_count, far_device),
        ]

        def sum_start(k, stage, value):
            buffer, send, recv, mine, count, device_of = stages[stage]
            buffer[k, mine] = value
            spread_start(buffer, send, recv, k, mine, count, device_of)

        def sum_end(k, stage):
            buffer, send, recv, mine, count, device_of = stages[stage]
            spread_wait(buffer, send, recv, k, mine, count, device_of)
            total = buffer[k, 0]
            for index in range(1, count):
                total = total + buffer[k, index]
            return total

        def weigh(vector):
            pieces = [vector[face * dofs : (face + 1) * dofs] * weights[face] for face in range(faces)]
            return jnp.concatenate(pieces, axis=0)

        def gather_start(k, weighted):
            gathered[k, coarse] = dot_left_transposed(basis_ref[...], weighted)

            def body(j, carry):
                index = (near + j) % near_count
                spread_copy(gathered, near_send, near_recv, k, coarse, near_device(index), coarse, index).start()
                return carry

            lax.fori_loop(1, near_count, body, 0)

        def gather_wait(k):
            def body(j, carry):
                index = (near + j) % near_count
                device = near_device(index)
                spread_copy(gathered, near_send, near_recv, k, coarse, device, device[0], index).wait_recv()
                return carry

            lax.fori_loop(1, near_count, body, 0)

        def gather_finish(k):
            def body(j, carry):
                index = (near + j) % near_count
                spread_copy(gathered, near_send, near_recv, k, coarse, near_device(index), coarse, index).wait_send()
                return carry

            lax.fori_loop(1, near_count, body, 0)

        def precondition(k, vector, target):
            weighted = weigh(vector)
            gather_start(k, weighted)
            solved = dot(inverse_ref[...], weighted)
            if k == 0:
                pair_copy(2, rows_ref, partner_rows).wait_recv()
            gather_wait(k)
            stacked = gathered[k].reshape(coarse_count * width, cases)
            part[k] = dot(partner_rows[...], stacked)
            pair = pair_copy(k, part.at[k], part_in.at[k])
            pair.start()
            own = dot(rows_ref[...], stacked)
            pair.wait_recv()
            combined = weigh(solved + dot(basis_ref[...], own + part_in[k]))
            target[...] = combined.reshape(faces, dofs, cases)
            return combined

        def column_sum(value):
            return jnp.sum(value, axis=0, keepdims=True)

        def flat(ref):
            return ref[...].reshape(order, cases)

        halo_start(0, loads_ref)
        pair_copy(2, rows_ref, partner_rows).start()
        halo_wait(0, loads_ref)
        r0 = flat(loads_ref) + flat(halo.at[0])
        u0 = precondition(0, r0, unsummed.at[0])
        halo_start(1, unsummed.at[0])
        gamma_part = column_sum(r0 * u0)
        halo_wait(1, unsummed.at[0])
        z0 = u0 + flat(halo.at[1])
        t0 = dot(operator_ref[...], z0)
        unsummed[1] = t0.reshape(faces, dofs, cases)
        halo_start(2, unsummed.at[1])
        pad = jnp.zeros((5, cases), jnp.float32)
        sum_start(0, 0, jnp.concatenate([gamma_part, column_sum(z0 * t0), pad, pad[:1]], axis=0))
        halo_wait(2, unsummed.at[1])
        q0 = t0 + flat(halo.at[2])
        sum_start(0, 1, sum_end(0, 0))
        u1 = precondition(1, q0, unsummed.at[2])
        halo_start(3, unsummed.at[2])
        sum_start(0, 2, sum_end(0, 1))
        halo_wait(3, unsummed.at[2])
        w0 = u1 + flat(halo.at[3])
        t1 = dot(operator_ref[...], w0)
        unsummed[3] = t1.reshape(faces, dofs, cases)
        halo_start(4, unsummed.at[3])
        first = sum_end(0, 2)
        gamma, energy = first[0:1], first[1:2]
        step = gamma / energy
        z1 = z0 - step * w0
        r1 = r0 - step * q0
        t1 = t0 - step * t1
        sum_start(
            1,
            0,
            jnp.concatenate(
                [column_sum(r1 * (u0 - step * u1)), column_sum(z1 * t1), column_sum(z0 * t1), pad], axis=0
            ),
        )
        sum_start(1, 1, sum_end(1, 0))
        sum_start(1, 2, sum_end(1, 1))
        halo_wait(4, unsummed.at[3])
        mapped = t1 + flat(halo.at[2]) - step * flat(halo.at[4])
        second = sum_end(1, 2)
        gamma_next = second[0:1]
        ratio = gamma_next / gamma
        last = gamma_next / (second[1:2] + 2.0 * ratio * second[2:3] + ratio * ratio * energy)
        solution_ref[...] = (step * z0 + last * (z1 + ratio * z0)).reshape(faces, dofs, cases)
        residual_ref[...] = (r1 - last * (mapped + ratio * q0)).reshape(faces, dofs, cases)

        halo_finish(0, loads_ref)
        for k in range(1, 5):
            halo_finish(k, unsummed.at[k - 1])
        pair_copy(2, rows_ref, partner_rows).wait_send()
        for k in range(2):
            gather_finish(k)
            pair_copy(k, part.at[k], part_in.at[k]).wait_send()
            for buffer, send, recv, mine, count, device_of in stages:
                spread_finish(buffer, send, recv, k, mine, count, device_of)

    return kernel


def in_vmem(count):
    return [pl.BlockSpec(memory_space=pltpu.VMEM)] * count


def on_device(sizes, face_loads, schur_blocks, coarse_basis, drop_masks, coarse_inverse):
    x_count, half_count, core_count, low_count, y_count, row_step = sizes
    coarse_count = x_count * half_count * core_count
    near_count, far_count = x_count * core_count, low_count * half_count
    faces, dofs, cases = face_loads.shape[2:]
    order = faces * dofs
    width = coarse_basis.shape[3]
    square = jax.ShapeDtypeStruct((order, order), jnp.float32)
    scaling = 1.0 + drop_masks.astype(jnp.float32)
    operator, inverse = pl.pallas_call(
        factor_kernel,
        out_shape=[square, square],
        in_specs=in_vmem(4),
        out_specs=in_vmem(2),
        scratch_shapes=[pltpu.VMEM((LEAF, LEAF), jnp.float32)],
        compiler_params=pltpu.CompilerParams(vmem_limit_bytes=16 << 20),
    )(schur_blocks[0, 0], coarse_basis[0, 0], scaling.reshape(order, 1), scaling.reshape(1, order))
    vector = jax.ShapeDtypeStruct((faces, dofs, cases), jnp.float32)
    dma = pltpu.SemaphoreType.DMA
    solved, residual = pl.pallas_call(
        make_iterate_kernel(sizes),
        out_shape=[vector, vector],
        in_specs=in_vmem(5),
        out_specs=in_vmem(2),
        scratch_shapes=[
            pltpu.VMEM((5, faces, dofs, cases), jnp.float32),
            pltpu.VMEM((4, faces, dofs, cases), jnp.float32),
            pltpu.VMEM((2, coarse_count, width, cases), jnp.float32),
            pltpu.VMEM((width, coarse_count * width), jnp.float32),
            pltpu.VMEM((2, width, cases), jnp.float32),
            pltpu.VMEM((2, width, cases), jnp.float32),
            pltpu.VMEM((2, near_count, 8, cases), jnp.float32),
            pltpu.VMEM((2, y_count, 8, cases), jnp.float32),
            pltpu.VMEM((2, far_count, 8, cases), jnp.float32),
            dma((5, faces)),
            dma((5, faces)),
            dma((2, near_count)),
            dma((2, coarse_count)),
            dma((3,)),
            dma((3,)),
            dma((2, near_count)),
            dma((2, near_count)),
            dma((2, y_count)),
            dma((2, y_count)),
            dma((2, far_count)),
            dma((2, far_count)),
        ],
        compiler_params=pltpu.CompilerParams(
            collective_id=0, has_side_effects=True, vmem_limit_bytes=32 << 20
        ),
    )(face_loads[0, 0], operator, inverse, coarse_basis[0, 0], coarse_inverse[0])
    return solved[None, None], residual[None, None]


def solution(mesh, sizes=(X_COUNT, HALF_COUNT, CORE_COUNT, LOW_COUNT, Y_COUNT, ROW)):
    def body(*arrays):
        return on_device(sizes, *arrays)

    return jax.shard_map(
        body,
        mesh=mesh,
        in_specs=(
            P("coarse", "sub", None, None, None),
            P("coarse", "sub", None, None),
            P("coarse", "sub", None, None),
            P("coarse", "sub", None, None),
            P("sub", "coarse", None),
        ),
        out_specs=(P("coarse", "sub", None, None, None), P("coarse", "sub", None, None, None)),
        check_vma=False,
    )
```

```python
import jax
import jax.numpy as jnp
from jax import lax
from jax.experimental import pallas as pl
from jax.experimental.pallas import tpu as pltpu
from jax.sharding import PartitionSpec as P

ROW = 8
X_COUNT, HALF_COUNT, CORE_COUNT = 4, 2, 2
LOW_COUNT, Y_COUNT = 8, 8
LEAF = 128
GROUP = 8

MESH = pl.DeviceIdType.MESH
highest = lax.Precision.HIGHEST


def dot(former, latter):
    return jnp.dot(former, latter, precision=highest, preferred_element_type=jnp.float32)


def dot_left_transposed(former, latter):
    return lax.dot_general(
        former, latter, (((0,), (0,)), ((), ())), precision=highest, preferred_element_type=jnp.float32
    )


def dot_right_transposed(former, latter):
    return lax.dot_general(
        former, latter, (((1,), (1,)), ((), ())), precision=highest, preferred_element_type=jnp.float32
    )


def reciprocal(value):
    guess = pl.reciprocal(value, approx=True)
    return guess * (2.0 - value * guess)


def product(former, latter):
    out = []
    for row in former:
        line = []
        for j in range(len(latter[0])):
            total = row[0] * latter[0][j]
            for t in range(1, len(latter)):
                total = total + row[t] * latter[t][j]
            line.append(total)
        out.append(line)
    return out


def small_inverse(matrix):
    size = len(matrix)
    if size == 2:
        a, b, c = matrix[0][0], matrix[0][1], matrix[1][1]
        det = reciprocal(a * c - b * b)
        return [[c * det, -b * det], [-b * det, a * det]]
    half = size // 2
    corner = [row[half:] for row in matrix[:half]]
    first = small_inverse([row[:half] for row in matrix[:half]])
    carried = product(first, corner)
    rest = [[None] * half for _ in range(half)]
    for i in range(half):
        for j in range(i, half):
            total = matrix[half + i][half + j]
            for t in range(half):
                total = total - corner[t][i] * carried[t][j]
            rest[i][j] = rest[j][i] = total
    second = small_inverse(rest)
    side = product(carried, second)
    out = [[None] * size for _ in range(size)]
    for i in range(half):
        for j in range(i, half):
            total = first[i][j]
            for t in range(half):
                total = total + side[i][t] * carried[j][t]
            out[i][j] = out[j][i] = total
        for j in range(half):
            out[i][half + j] = out[half + j][i] = -side[i][j]
            out[half + i][half + j] = second[i][j]
    return out


def invert_leaf(leaf_ref, panel_ref, entry_ref):
    shape = (GROUP, LEAF)
    lane = lax.broadcasted_iota(jnp.int32, shape, 1)
    sublane = lax.broadcasted_iota(jnp.int32, shape, 0)
    wide_lane = lax.broadcasted_iota(jnp.int32, (LEAF, LEAF), 1)
    last = LEAF - GROUP

    def solve(panel):
        for s in range(GROUP):
            entry_ref[s] = jnp.broadcast_to(panel[:, s : s + 1], shape)
        pivots = [[None] * GROUP for _ in range(GROUP)]
        for r in range(GROUP):
            for s in range(r, GROUP):
                pivots[r][s] = pivots[s][r] = jnp.broadcast_to(entry_ref[s, r : r + 1, :], shape)
        inverse = small_inverse(pivots)
        turned = jnp.where(lane >= last, 0.0, pltpu.roll(panel, last, 1))
        panel_ref[...] = jnp.where(lane == last + sublane, 1.0, turned)
        unit = [jnp.broadcast_to(panel_ref[t : t + 1, :], shape) for t in range(GROUP)]
        solved = []
        for s in range(GROUP):
            total = inverse[s][0] * unit[0]
            for t in range(1, GROUP):
                total = total + inverse[s][t] * unit[t]
            solved.append(total)
        return solved

    def tile_of(solved):
        tile = solved[0]
        for s in range(1, GROUP):
            tile = jnp.where(sublane == s, solved[s], tile)
        return tile

    def update(tile):
        old = leaf_ref[...]
        turned = jnp.where(wide_lane >= last, 0.0, pltpu.roll(old, last, 1))
        return turned - dot(old[:, :GROUP], tile)

    def step(g, solved):
        tile = tile_of(solved)
        old = leaf_ref[pl.ds(pl.multiple_of((g + 1) * GROUP, GROUP), GROUP), :]
        panel = jnp.where(lane >= last, 0.0, pltpu.roll(old, last, 1))
        for s in range(GROUP):
            panel = panel - jnp.broadcast_to(old[:, s : s + 1], shape) * solved[s]
        following = solve(panel)
        new = update(tile)
        for i in range(LEAF // GROUP):
            rows = slice(i * GROUP, (i + 1) * GROUP)
            leaf_ref[rows, :] = jnp.where(g == i, tile, jnp.where(g + 1 == i, panel, new[rows]))
        return following

    solved = lax.fori_loop(0, LEAF // GROUP - 1, step, solve(leaf_ref[:GROUP, :]))
    new = update(tile_of(solved))
    leaf_ref[:last, :] = new[:last]
    leaf_ref[last:, :] = tile_of(solved)


def eliminate(matrix_ref, leaf_ref, panel_ref, entry_ref, j):
    blocks = matrix_ref.shape[0] // LEAF
    here = slice(j * LEAF, (j + 1) * LEAF)
    leaf_ref[...] = matrix_ref[here, here]
    invert_leaf(leaf_ref, panel_ref, entry_ref)
    inverse = leaf_ref[...]
    matrix_ref[here, here] = inverse
    others = [slice(i * LEAF, (i + 1) * LEAF) for i in range(blocks) if i != j]
    for columns in others:
        matrix_ref[here, columns] = dot(inverse, matrix_ref[here, columns])
    for rows in others:
        column = matrix_ref[rows, here]
        for columns in others:
            matrix_ref[rows, columns] = matrix_ref[rows, columns] - dot(column, matrix_ref[here, columns])
        matrix_ref[rows, here] = -dot(column, inverse)


def make_iterate_kernel(sizes):
    x_count, half_count, core_count, low_count, y_count, row_step = sizes
    coarse_count = x_count * half_count * core_count
    sub_count = low_count * y_count
    near_count = x_count * core_count
    far_count = low_count * half_count

    def kernel(
        loads_hbm, schur_hbm, basis_hbm, masks_ref, rows_hbm, solution_ref, residual_ref,
        loads_ref, operator_ref, basis_ref, rows_ref, inverse_ref, leaf_ref, panel_ref, entry_ref,
        halo, unsummed, gathered, partner_rows, part, part_in, sums_1a, sums_1b, sums_1c, sums_2a, sums_2b, sums_2c,
        own_sem,
        halo_send, halo_recv, near_send, near_recv, pair_send, pair_recv,
        a_send, a_recv, b_send, b_recv, c_send, c_recv,
    ):
        faces, dofs, cases = loads_ref.shape
        order = faces * dofs
        width = basis_ref.shape[1]
        coarse = lax.axis_index("coarse")
        sub = lax.axis_index("sub")
        core = coarse % core_count
        half = (coarse // core_count) % half_count
        x = coarse // (core_count * half_count)
        y = sub % y_count
        low = sub // y_count
        near = x * core_count + core
        far = low * half_count + half

        def near_device(index):
            return ((index // core_count * half_count + half) * core_count + index % core_count, sub)

        def y_device(index):
            return (coarse, low * y_count + index)

        def far_device(index):
            return ((x * half_count + index % half_count) * core_count + core, index // half_count * y_count + y)

        partner = ((x * half_count + (half_count - 1 - half)) * core_count + core, sub)
        present = [
            coarse > 0,
            coarse < coarse_count - 1,
            sub > 0,
            sub < sub_count - 1,
            sub >= row_step,
            sub < sub_count - row_step,
        ]
        neighbour = [
            (coarse - 1, sub),
            (coarse + 1, sub),
            (coarse, sub - 1),
            (coarse, sub + 1),
            (coarse, sub - row_step),
            (coarse, sub + row_step),
        ]

        own = []
        for n, (source, target) in enumerate(
            [(loads_hbm, loads_ref), (schur_hbm, operator_ref), (basis_hbm, basis_ref), (rows_hbm, rows_ref)]
        ):
            own.append(pltpu.make_async_copy(source, target, own_sem.at[n]))
            own[n].start()

        barrier = pltpu.get_barrier_semaphore()

        def greet(device):
            pl.semaphore_signal(barrier, inc=1, device_id=device, device_id_type=MESH)

        lax.fori_loop(1, near_count, lambda j, c: (greet(near_device((near + j) % near_count)), c)[1], 0)
        lax.fori_loop(1, y_count, lambda j, c: (greet(y_device((y + j) % y_count)), c)[1], 0)
        lax.fori_loop(1, far_count, lambda j, c: (greet(far_device((far + j) % far_count)), c)[1], 0)
        expected = near_count + y_count + far_count - 3
        for face in range(faces):
            expected = expected + present[face].astype(jnp.int32)

            @pl.when(present[face])
            def _():
                greet(neighbour[face])

        weights = [jnp.where(present[face], 0.5, 1.0) for face in range(faces)]
        for face in range(faces):

            @pl.when(jnp.logical_not(present[face]))
            def _():
                for k in range(halo.shape[0]):
                    halo[k, face] = jnp.zeros((dofs, cases), jnp.float32)

        for k in range(gathered.shape[0]):
            for index in range(near_count):
                place = (index // core_count * half_count + (half_count - 1 - half)) * core_count + index % core_count
                gathered[k, place] = jnp.zeros(gathered.shape[2:], jnp.float32)
        own[0].wait()
        own[3].wait()
        pl.semaphore_wait(barrier, expected)

        def halo_copy(k, source, face):
            return pltpu.make_async_remote_copy(
                src_ref=source.at[face],
                dst_ref=halo.at[k, face ^ 1],
                send_sem=halo_send.at[k, face],
                recv_sem=halo_recv.at[k, face ^ 1],
                device_id=neighbour[face],
                device_id_type=MESH,
            )

        def halo_start(k, source):
            for face in range(faces):

                @pl.when(present[face])
                def _():
                    halo_copy(k, source, face).start()

        def halo_wait(k, source):
            for face in range(faces):

                @pl.when(present[face])
                def _():
                    halo_copy(k, source, face ^ 1).wait_recv()

        def halo_finish(k, source):
            for face in range(faces):

                @pl.when(present[face])
                def _():
                    halo_copy(k, source, face).wait_send()

        def pair_copy(k, source, target):
            return pltpu.make_async_remote_copy(
                src_ref=source,
                dst_ref=target,
                send_sem=pair_send.at[k],
                recv_sem=pair_recv.at[k],
                device_id=partner,
                device_id_type=MESH,
            )

        def spread_copy(buffer, send, recv, k, mine, device, slot, index):
            return pltpu.make_async_remote_copy(
                src_ref=buffer.at[mine],
                dst_ref=buffer.at[slot],
                send_sem=send.at[k, index],
                recv_sem=recv.at[k, slot],
                device_id=device,
                device_id_type=MESH,
            )

        def spread_start(buffer, send, recv, k, mine, count, device_of):
            def body(j, carry):
                index = (mine + j) % count
                spread_copy(buffer, send, recv, k, mine, device_of(index), mine, index).start()
                return carry

            lax.fori_loop(1, count, body, 0)

        def spread_wait(buffer, send, recv, k, mine, count, device_of):
            def body(j, carry):
                index = (mine + j) % count
                spread_copy(buffer, send, recv, k, mine, device_of(index), index, index).wait_recv()
                return carry

            lax.fori_loop(1, count, body, 0)

        def spread_finish(buffer, send, recv, k, mine, count, device_of):
            def body(j, carry):
                index = (mine + j) % count
                spread_copy(buffer, send, recv, k, mine, device_of(index), mine, index).wait_send()
                return carry

            lax.fori_loop(1, count, body, 0)

        stages = [
            ((sums_1a, sums_2a), a_send, a_recv, near, near_count, near_device),
            ((sums_1b, sums_2b), b_send, b_recv, y, y_count, y_device),
            ((sums_1c, sums_2c), c_send, c_recv, far, far_count, far_device),
        ]

        def sum_start(k, stage, value):
            buffers, send, recv, mine, count, device_of = stages[stage]
            buffer = buffers[k]
            buffer[mine] = value
            spread_start(buffer, send, recv, k, mine, count, device_of)

        def sum_end(k, stage):
            buffers, send, recv, mine, count, device_of = stages[stage]
            buffer = buffers[k]
            spread_wait(buffer, send, recv, k, mine, count, device_of)
            total = buffer[0]
            for index in range(1, count):
                total = total + buffer[index]
            return total

        def weigh(vector):
            pieces = [vector[face * dofs : (face + 1) * dofs] * weights[face] for face in range(faces)]
            return jnp.concatenate(pieces, axis=0)

        def gather_start(k, weighted):
            gathered[k, coarse] = dot_left_transposed(basis_ref[...], weighted)

            def body(j, carry):
                index = (near + j) % near_count
                spread_copy(gathered.at[k], near_send, near_recv, k, coarse, near_device(index), coarse, index).start()
                return carry

            lax.fori_loop(1, near_count, body, 0)

        def gather_wait(k):
            def body(j, carry):
                index = (near + j) % near_count
                device = near_device(index)
                spread_copy(gathered.at[k], near_send, near_recv, k, coarse, device, device[0], index).wait_recv()
                return carry

            lax.fori_loop(1, near_count, body, 0)

        def gather_finish(k):
            def body(j, carry):
                index = (near + j) % near_count
                spread_copy(gathered.at[k], near_send, near_recv, k, coarse, near_device(index), coarse, index).wait_send()
                return carry

            lax.fori_loop(1, near_count, body, 0)

        def coarse_start(k):
            gather_wait(k)
            stacked = gathered[k].reshape(coarse_count * width, cases)
            part[k] = dot(partner_rows[...], stacked)
            pair_copy(k, part.at[k], part_in.at[k]).start()
            return dot(rows_ref[...], stacked)

        def precondition(k, solved, coarse_part, target):
            pair_copy(k, part.at[k], part_in.at[k]).wait_recv()
            combined = weigh(solved + dot(basis_ref[...], coarse_part + part_in[k]))
            target[...] = combined.reshape(faces, dofs, cases)
            return combined

        def invert_block(j):
            eliminate(inverse_ref, leaf_ref, panel_ref, entry_ref, j)

        def column_sum(value):
            return jnp.sum(value, axis=0, keepdims=True)

        def flat(ref):
            return ref[...].reshape(order, cases)

        halo_start(0, loads_ref)
        pair_copy(2, rows_ref, partner_rows).start()
        own[1].wait()
        own[2].wait()
        scaling = 1.0 + masks_ref[...].astype(jnp.float32)
        faces_in_leaf = LEAF // dofs
        diagonal = lax.broadcasted_iota(jnp.int32, (LEAF, LEAF), 0) == lax.broadcasted_iota(
            jnp.int32, (LEAF, LEAF), 1
        )
        blocks = [slice(i * LEAF, (i + 1) * LEAF) for i in range(order // LEAF)]
        across = [
            jnp.concatenate([scaling[i * faces_in_leaf + f : i * faces_in_leaf + f + 1] for f in range(faces_in_leaf)], axis=1)
            for i in range(len(blocks))
        ]
        for i, rows in enumerate(blocks):
            down = jnp.sum(jnp.where(diagonal, across[i], 0.0), axis=1, keepdims=True)
            for j, columns in enumerate(blocks):
                operator_ref[rows, columns] = down * operator_ref[rows, columns] * across[j]
        inverse_ref[...] = operator_ref[...] + dot_right_transposed(basis_ref[...], basis_ref[...])
        invert_block(0)
        halo_wait(0, loads_ref)
        r0 = flat(loads_ref) + flat(halo.at[0])
        weighted = weigh(r0)
        gather_start(0, weighted)
        invert_block(1)
        pair_copy(2, rows_ref, partner_rows).wait_recv()
        coarse_part = coarse_start(0)
        invert_block(2)
        u0 = precondition(0, dot(inverse_ref[...], weighted), coarse_part, unsummed.at[0])
        halo_start(1, unsummed.at[0])
        gamma_part = column_sum(r0 * u0)
        halo_wait(1, unsummed.at[0])
        z0 = u0 + flat(halo.at[1])
        t0 = dot(operator_ref[...], z0)
        unsummed[1] = t0.reshape(faces, dofs, cases)
        halo_start(2, unsummed.at[1])
        sum_start(0, 0, jnp.concatenate([gamma_part, column_sum(z0 * t0)], axis=0))
        halo_wait(2, unsummed.at[1])
        q0 = t0 + flat(halo.at[2])
        weighted = weigh(q0)
        gather_start(1, weighted)
        solved = dot(inverse_ref[...], weighted)
        sum_start(0, 1, sum_end(0, 0))
        coarse_part = coarse_start(1)
        u1 = precondition(1, solved, coarse_part, unsummed.at[2])
        halo_start(3, unsummed.at[2])
        sum_start(0, 2, sum_end(0, 1))
        halo_wait(3, unsummed.at[2])
        w0 = u1 + flat(halo.at[3])
        t1 = dot(operator_ref[...], w0)
        unsummed[3] = t1.reshape(faces, dofs, cases)
        halo_start(4, unsummed.at[3])
        first = sum_end(0, 2)
        gamma, energy = first[0:1], first[1:2]
        step = gamma / energy
        z1 = z0 - step * w0
        r1 = r0 - step * q0
        t1 = t0 - step * t1
        sum_start(
            1,
            0,
            jnp.concatenate(
                [column_sum(r1 * (u0 - step * u1)), column_sum(z1 * t1), column_sum(z0 * t1), jnp.zeros_like(step)],
                axis=0,
            ),
        )
        sum_start(1, 1, sum_end(1, 0))
        sum_start(1, 2, sum_end(1, 1))
        halo_wait(4, unsummed.at[3])
        mapped = t1 + flat(halo.at[2]) - step * flat(halo.at[4])
        second = sum_end(1, 2)
        gamma_next = second[0:1]
        ratio = gamma_next / gamma
        last = gamma_next / (second[1:2] + 2.0 * ratio * second[2:3] + ratio * ratio * energy)
        solution_ref[...] = (step * z0 + last * (z1 + ratio * z0)).reshape(faces, dofs, cases)
        residual_ref[...] = (r1 - last * (mapped + ratio * q0)).reshape(faces, dofs, cases)

        halo_finish(0, loads_ref)
        for k in range(1, 5):
            halo_finish(k, unsummed.at[k - 1])
        pair_copy(2, rows_ref, partner_rows).wait_send()
        for k in range(2):
            gather_finish(k)
            pair_copy(k, part.at[k], part_in.at[k]).wait_send()
            for buffers, send, recv, mine, count, device_of in stages:
                spread_finish(buffers[k], send, recv, k, mine, count, device_of)

    return kernel


def on_device(sizes, face_loads, schur_blocks, coarse_basis, drop_masks, coarse_inverse):
    x_count, half_count, core_count, low_count, y_count, row_step = sizes
    coarse_count = x_count * half_count * core_count
    near_count, far_count = x_count * core_count, low_count * half_count
    faces, dofs, cases = face_loads.shape[2:]
    order = faces * dofs
    width = coarse_basis.shape[3]
    vector = jax.ShapeDtypeStruct((faces, dofs, cases), jnp.float32)
    dma = pltpu.SemaphoreType.DMA
    solved, residual = pl.pallas_call(
        make_iterate_kernel(sizes),
        out_shape=[vector, vector],
        in_specs=[
            pl.BlockSpec(memory_space=pl.ANY),
            pl.BlockSpec(memory_space=pl.ANY),
            pl.BlockSpec(memory_space=pl.ANY),
            pl.BlockSpec(memory_space=pltpu.VMEM),
            pl.BlockSpec(memory_space=pl.ANY),
        ],
        out_specs=[pl.BlockSpec(memory_space=pltpu.VMEM)] * 2,
        scratch_shapes=[
            pltpu.VMEM((faces, dofs, cases), jnp.float32),
            pltpu.VMEM((order, order), jnp.float32),
            pltpu.VMEM((order, width), jnp.float32),
            pltpu.VMEM((width, coarse_count * width), jnp.float32),
            pltpu.VMEM((order, order), jnp.float32),
            pltpu.VMEM((LEAF, LEAF), jnp.float32),
            pltpu.VMEM((GROUP, LEAF), jnp.float32),
            pltpu.VMEM((GROUP, GROUP, LEAF), jnp.float32),
            pltpu.VMEM((5, faces, dofs, cases), jnp.float32),
            pltpu.VMEM((4, faces, dofs, cases), jnp.float32),
            pltpu.VMEM((2, coarse_count, width, cases), jnp.float32),
            pltpu.VMEM((width, coarse_count * width), jnp.float32),
            pltpu.VMEM((2, width, cases), jnp.float32),
            pltpu.VMEM((2, width, cases), jnp.float32),
            pltpu.VMEM((near_count, 2, cases), jnp.float32),
            pltpu.VMEM((y_count, 2, cases), jnp.float32),
            pltpu.VMEM((far_count, 2, cases), jnp.float32),
            pltpu.VMEM((near_count, 4, cases), jnp.float32),
            pltpu.VMEM((y_count, 4, cases), jnp.float32),
            pltpu.VMEM((far_count, 4, cases), jnp.float32),
            dma((4,)),
            dma((5, faces)),
            dma((5, faces)),
            dma((2, near_count)),
            dma((2, coarse_count)),
            dma((3,)),
            dma((3,)),
            dma((2, near_count)),
            dma((2, near_count)),
            dma((2, y_count)),
            dma((2, y_count)),
            dma((2, far_count)),
            dma((2, far_count)),
        ],
        compiler_params=pltpu.CompilerParams(
            collective_id=0, has_side_effects=True, vmem_limit_bytes=32 << 20
        ),
    )(face_loads[0, 0], schur_blocks[0, 0], coarse_basis[0, 0], drop_masks[0, 0], coarse_inverse[0])
    return solved[None, None], residual[None, None]


def solution(mesh, sizes=(X_COUNT, HALF_COUNT, CORE_COUNT, LOW_COUNT, Y_COUNT, ROW)):
    def body(*arrays):
        return on_device(sizes, *arrays)

    return jax.shard_map(
        body,
        mesh=mesh,
        in_specs=(
            P("coarse", "sub", None, None, None),
            P("coarse", "sub", None, None),
            P("coarse", "sub", None, None),
            P("coarse", "sub", None, None),
            P("sub", "coarse", None),
        ),
        out_specs=(P("coarse", "sub", None, None, None), P("coarse", "sub", None, None, None)),
        check_vma=False,
    )
```

```python
import jax
import jax.numpy as jnp
from jax import lax
from jax.experimental import pallas as pl
from jax.experimental.pallas import tpu as pltpu
from jax.sharding import PartitionSpec as P

ROW = 8
X_COUNT, HALF_COUNT, CORE_COUNT = 4, 2, 2
LOW_COUNT, Y_COUNT = 8, 8
LEAF = 128
GROUP = 8

MESH = pl.DeviceIdType.MESH
highest = lax.Precision.HIGHEST


def dot(former, latter):
    return jnp.dot(former, latter, precision=highest, preferred_element_type=jnp.float32)


def dot_left_transposed(former, latter):
    return lax.dot_general(
        former, latter, (((0,), (0,)), ((), ())), precision=highest, preferred_element_type=jnp.float32
    )


def reciprocal(value):
    guess = pl.reciprocal(value, approx=True)
    return guess * (2.0 - value * guess)


def product(former, latter):
    out = []
    for row in former:
        line = []
        for j in range(len(latter[0])):
            total = row[0] * latter[0][j]
            for t in range(1, len(latter)):
                total = total + row[t] * latter[t][j]
            line.append(total)
        out.append(line)
    return out


def small_inverse(matrix):
    size = len(matrix)
    if size == 2:
        a, b, c = matrix[0][0], matrix[0][1], matrix[1][1]
        det = reciprocal(a * c - b * b)
        return [[c * det, -b * det], [-b * det, a * det]]
    first, carried, second = halves(matrix)
    half = size // 2
    side = product(carried, second)
    out = [[None] * size for _ in range(size)]
    for i in range(half):
        for j in range(i, half):
            total = first[i][j]
            for t in range(half):
                total = total + side[i][t] * carried[j][t]
            out[i][j] = out[j][i] = total
        for j in range(half):
            out[i][half + j] = out[half + j][i] = -side[i][j]
            out[half + i][half + j] = second[i][j]
    return out


def halves(matrix):
    half = len(matrix) // 2
    corner = [row[half:] for row in matrix[:half]]
    first = small_inverse([row[:half] for row in matrix[:half]])
    carried = product(first, corner)
    rest = [[None] * half for _ in range(half)]
    for i in range(half):
        for j in range(i, half):
            total = matrix[half + i][half + j]
            for t in range(half):
                total = total - corner[t][i] * carried[t][j]
            rest[i][j] = rest[j][i] = total
    return first, carried, small_inverse(rest)


def small_solve(matrix, right):
    half = len(matrix) // 2
    first, carried, second = halves(matrix)
    lower = []
    for i in range(half):
        total = right[half + i]
        for t in range(half):
            total = total - carried[t][i] * right[t]
        lower.append(total)
    upper = [row[0] for row in product(first, [[value] for value in right[:half]])]
    below = [row[0] for row in product(second, [[value] for value in lower])]
    above = []
    for i in range(half):
        total = upper[i]
        for t in range(half):
            total = total - carried[i][t] * below[t]
        above.append(total)
    return above + below


def invert_leaf(leaf_ref, panel_ref, entry_ref):
    shape = (GROUP, LEAF)
    lane = lax.broadcasted_iota(jnp.int32, shape, 1)
    sublane = lax.broadcasted_iota(jnp.int32, shape, 0)
    wide_lane = lax.broadcasted_iota(jnp.int32, (LEAF, LEAF), 1)
    last = LEAF - GROUP

    def solve(panel):
        for s in range(GROUP):
            entry_ref[s] = jnp.broadcast_to(panel[:, s : s + 1], shape)
        pivots = [[None] * GROUP for _ in range(GROUP)]
        for r in range(GROUP):
            for s in range(r, GROUP):
                pivots[r][s] = pivots[s][r] = jnp.broadcast_to(entry_ref[s, r : r + 1, :], shape)
        turned = jnp.where(lane >= last, 0.0, pltpu.roll(panel, last, 1))
        panel_ref[...] = jnp.where(lane == last + sublane, 1.0, turned)
        unit = [jnp.broadcast_to(panel_ref[t : t + 1, :], shape) for t in range(GROUP)]
        return small_solve(pivots, unit)

    def tile_of(solved):
        tile = solved[0]
        for s in range(1, GROUP):
            tile = jnp.where(sublane == s, solved[s], tile)
        return tile

    def update(tile):
        old = leaf_ref[...]
        turned = jnp.where(wide_lane >= last, 0.0, pltpu.roll(old, last, 1))
        return turned - dot(old[:, :GROUP], tile)

    def step(g, solved):
        tile = tile_of(solved)
        old = leaf_ref[pl.ds(pl.multiple_of((g + 1) * GROUP, GROUP), GROUP), :]
        panel = jnp.where(lane >= last, 0.0, pltpu.roll(old, last, 1))
        for s in range(GROUP):
            panel = panel - jnp.broadcast_to(old[:, s : s + 1], shape) * solved[s]
        following = solve(panel)
        new = update(tile)
        for i in range(LEAF // GROUP):
            rows = slice(i * GROUP, (i + 1) * GROUP)
            leaf_ref[rows, :] = jnp.where(g == i, tile, jnp.where(g + 1 == i, panel, new[rows]))
        return following

    solved = lax.fori_loop(0, LEAF // GROUP - 1, step, solve(leaf_ref[:GROUP, :]))
    new = update(tile_of(solved))
    leaf_ref[:last, :] = new[:last]
    leaf_ref[last:, :] = tile_of(solved)


def eliminate(matrix_ref, leaf_ref, panel_ref, entry_ref, j):
    blocks = matrix_ref.shape[0] // LEAF
    here = slice(j * LEAF, (j + 1) * LEAF)
    leaf_ref[...] = matrix_ref[here, here]
    invert_leaf(leaf_ref, panel_ref, entry_ref)
    inverse = leaf_ref[...]
    matrix_ref[here, here] = inverse
    others = [slice(i * LEAF, (i + 1) * LEAF) for i in range(blocks) if i != j]
    for columns in others:
        matrix_ref[here, columns] = dot(inverse, matrix_ref[here, columns])
    for rows in others:
        column = matrix_ref[rows, here]
        for columns in others:
            matrix_ref[rows, columns] = matrix_ref[rows, columns] - dot(column, matrix_ref[here, columns])
        matrix_ref[rows, here] = -dot(column, inverse)


def make_iterate_kernel(sizes):
    x_count, half_count, core_count, low_count, y_count, row_step = sizes
    coarse_count = x_count * half_count * core_count
    sub_count = low_count * y_count
    near_count = x_count * core_count
    far_count = low_count * half_count

    def kernel(
        loads_hbm, schur_hbm, basis_hbm, masks_ref, rows_hbm, solution_ref, residual_ref,
        loads_ref, operator_ref, basis_ref, rows_ref, inverse_ref, leaf_ref, panel_ref, entry_ref,
        halo, unsummed, gathered, partner_rows, part, part_in,
        far_out, corner_out, corner_in, slice_out, slice_in, far_rows, own_out, own_in,
        sums_1a, sums_1b, sums_1c, sums_2a, sums_2b, sums_2c,
        own_sem, far_send, far_recv,
        halo_send, halo_recv, near_send, near_recv, pair_send, pair_recv,
        a_send, a_recv, b_send, b_recv, c_send, c_recv,
    ):
        faces, dofs, cases = loads_ref.shape
        order = faces * dofs
        width = basis_ref.shape[0]
        coarse = lax.axis_index("coarse")
        sub = lax.axis_index("sub")
        core = coarse % core_count
        half = (coarse // core_count) % half_count
        x = coarse // (core_count * half_count)
        y = sub % y_count
        low = sub // y_count
        near = x * core_count + core
        far = low * half_count + half

        def near_device(index):
            return ((index // core_count * half_count + half) * core_count + index % core_count, sub)

        def y_device(index):
            return (coarse, low * y_count + index)

        def far_device(index):
            return ((x * half_count + index % half_count) * core_count + core, index // half_count * y_count + y)

        partner = ((x * half_count + (half_count - 1 - half)) * core_count + core, sub)
        present = [
            coarse > 0,
            coarse < coarse_count - 1,
            sub > 0,
            sub < sub_count - 1,
            sub >= row_step,
            sub < sub_count - row_step,
        ]
        neighbour = [
            (coarse - 1, sub),
            (coarse + 1, sub),
            (coarse, sub - 1),
            (coarse, sub + 1),
            (coarse, sub - row_step),
            (coarse, sub + row_step),
        ]

        own = []
        for n, (source, target) in enumerate(
            [(loads_hbm, loads_ref), (schur_hbm, operator_ref), (basis_hbm, basis_ref), (rows_hbm, rows_ref)]
        ):
            own.append(pltpu.make_async_copy(source, target, own_sem.at[n]))
            own[n].start()

        barrier = pltpu.get_barrier_semaphore()

        def greet(device):
            pl.semaphore_signal(barrier, inc=1, device_id=device, device_id_type=MESH)

        lax.fori_loop(1, near_count, lambda j, c: (greet(near_device((near + j) % near_count)), c)[1], 0)
        lax.fori_loop(1, y_count, lambda j, c: (greet(y_device((y + j) % y_count)), c)[1], 0)
        lax.fori_loop(1, far_count, lambda j, c: (greet(far_device((far + j) % far_count)), c)[1], 0)
        expected = near_count + y_count + far_count - 3
        for face in range(faces):
            expected = expected + present[face].astype(jnp.int32)

            @pl.when(present[face])
            def _():
                greet(neighbour[face])

        weights = [jnp.where(present[face], 0.5, 1.0) for face in range(faces)]
        for face in range(faces):

            @pl.when(jnp.logical_not(present[face]))
            def _():
                for k in range(halo.shape[0]):
                    halo[k, face] = jnp.zeros((dofs, cases), jnp.float32)

        for k in range(gathered.shape[0]):
            for index in range(near_count):
                place = (index // core_count * half_count + (half_count - 1 - half)) * core_count + index % core_count
                gathered[k, place] = jnp.zeros(gathered.shape[2:], jnp.float32)
        own[0].wait()
        own[3].wait()
        pl.semaphore_wait(barrier, expected)

        far_present = jnp.logical_or(
            jnp.logical_and(core == 0, present[0]), jnp.logical_and(core == 1, present[1])
        )
        far_device_id = (coarse - 1 + 2 * core, sub)

        @pl.when(jnp.logical_not(far_present))
        def _():
            for buffer in (corner_in, slice_in, far_rows, own_in):
                buffer[...] = jnp.zeros_like(buffer)

        def face_copy(k, source, face, device):
            return pltpu.make_async_remote_copy(
                src_ref=source,
                dst_ref=halo.at[k, face ^ 1],
                send_sem=halo_send.at[k, face],
                recv_sem=halo_recv.at[k, face ^ 1],
                device_id=device,
                device_id_type=MESH,
            )

        def near_faces(action):
            for face in range(faces):
                here = present[face]
                if face < 2:
                    here = jnp.logical_and(here, core != face)

                @pl.when(here)
                def _():
                    action(face)

        def near_start(k, source):
            near_faces(lambda face: face_copy(k, source.at[face], face, neighbour[face]).start())

        def near_wait(k):
            near_faces(lambda face: face_copy(k, halo.at[k, face], face ^ 1, neighbour[face]).wait_recv())

        def near_finish(k, source):
            near_faces(lambda face: face_copy(k, source.at[face], face, neighbour[face]).wait_send())

        def far_face_copy(k, source):
            return pltpu.make_async_remote_copy(
                src_ref=source,
                dst_ref=halo.at[k, 1 - core],
                send_sem=halo_send.at[k, core],
                recv_sem=halo_recv.at[k, 1 - core],
                device_id=far_device_id,
                device_id_type=MESH,
            )

        def far_face_start(k, source):
            @pl.when(far_present)
            def _():
                far_face_copy(k, source).start()

        def far_face_wait(k):
            @pl.when(far_present)
            def _():
                pltpu.make_async_remote_copy(
                    src_ref=halo.at[k, core],
                    dst_ref=halo.at[k, core],
                    send_sem=halo_send.at[k, 1 - core],
                    recv_sem=halo_recv.at[k, core],
                    device_id=far_device_id,
                    device_id_type=MESH,
                ).wait_recv()

        def far_face_finish(k, source):
            @pl.when(far_present)
            def _():
                far_face_copy(k, source).wait_send()

        def far_copy(n, source, target):
            return pltpu.make_async_remote_copy(
                src_ref=source,
                dst_ref=target,
                send_sem=far_send.at[n],
                recv_sem=far_recv.at[n],
                device_id=far_device_id,
                device_id_type=MESH,
            )

        far_pairs = [(rows_ref, far_rows), (corner_out, corner_in), (slice_out, slice_in), (own_out, own_in)]

        def far_start(n):
            @pl.when(far_present)
            def _():
                far_copy(n, *far_pairs[n]).start()

        def far_wait(n):
            @pl.when(far_present)
            def _():
                far_copy(n, *far_pairs[n]).wait_recv()

        def far_finish(n):
            @pl.when(far_present)
            def _():
                far_copy(n, *far_pairs[n]).wait_send()

        def near_incoming(k):
            sibling = halo[k, 1 - core]
            pieces = [jnp.where(core == 1, sibling, 0.0), jnp.where(core == 0, sibling, 0.0)]
            return jnp.concatenate(pieces + [halo[k, face] for face in range(2, faces)], axis=0)

        def on_far_face(value):
            return jnp.concatenate([jnp.where(core == 0, value, 0.0), jnp.where(core == 1, value, 0.0)], axis=0)

        def far_face_of(value):
            return jnp.where(core == 0, value[:dofs], value[dofs : 2 * dofs])

        def add_on_coarse_faces(value, extra):
            return jnp.concatenate([value[: 2 * dofs] + extra, value[2 * dofs :]], axis=0)

        def pair_copy(k, source, target):
            return pltpu.make_async_remote_copy(
                src_ref=source,
                dst_ref=target,
                send_sem=pair_send.at[k],
                recv_sem=pair_recv.at[k],
                device_id=partner,
                device_id_type=MESH,
            )

        def spread_copy(buffer, send, recv, k, mine, device, slot, index):
            return pltpu.make_async_remote_copy(
                src_ref=buffer.at[mine],
                dst_ref=buffer.at[slot],
                send_sem=send.at[k, index],
                recv_sem=recv.at[k, slot],
                device_id=device,
                device_id_type=MESH,
            )

        def spread_start(buffer, send, recv, k, mine, count, device_of):
            def body(j, carry):
                index = (mine + j) % count
                spread_copy(buffer, send, recv, k, mine, device_of(index), mine, index).start()
                return carry

            lax.fori_loop(1, count, body, 0)

        def spread_wait(buffer, send, recv, k, mine, count, device_of):
            def body(j, carry):
                index = (mine + j) % count
                spread_copy(buffer, send, recv, k, mine, device_of(index), index, index).wait_recv()
                return carry

            lax.fori_loop(1, count, body, 0)

        def spread_finish(buffer, send, recv, k, mine, count, device_of):
            def body(j, carry):
                index = (mine + j) % count
                spread_copy(buffer, send, recv, k, mine, device_of(index), mine, index).wait_send()
                return carry

            lax.fori_loop(1, count, body, 0)

        stages = [
            ((sums_1a, sums_2a), a_send, a_recv, near, near_count, near_device),
            ((sums_1b, sums_2b), b_send, b_recv, y, y_count, y_device),
            ((sums_1c, sums_2c), c_send, c_recv, far, far_count, far_device),
        ]

        def sum_start(k, stage, value):
            buffers, send, recv, mine, count, device_of = stages[stage]
            buffer = buffers[k]
            buffer[mine] = value
            spread_start(buffer, send, recv, k, mine, count, device_of)

        def sum_end(k, stage):
            buffers, send, recv, mine, count, device_of = stages[stage]
            buffer = buffers[k]
            spread_wait(buffer, send, recv, k, mine, count, device_of)
            total = buffer[0]
            for index in range(1, count):
                total = total + buffer[index]
            return total

        def weigh(vector):
            pieces = [vector[face * dofs : (face + 1) * dofs] * weights[face] for face in range(faces)]
            return jnp.concatenate(pieces, axis=0)

        def gather_start(k, weighted):
            gathered[k, coarse] = dot(basis_ref[...], weighted)

            def body(j, carry):
                index = (near + j) % near_count
                spread_copy(gathered.at[k], near_send, near_recv, k, coarse, near_device(index), coarse, index).start()
                return carry

            lax.fori_loop(1, near_count, body, 0)

        def gather_wait(k):
            def body(j, carry):
                index = (near + j) % near_count
                device = near_device(index)
                spread_copy(gathered.at[k], near_send, near_recv, k, coarse, device, device[0], index).wait_recv()
                return carry

            lax.fori_loop(1, near_count, body, 0)

        def gather_finish(k):
            def body(j, carry):
                index = (near + j) % near_count
                spread_copy(gathered.at[k], near_send, near_recv, k, coarse, near_device(index), coarse, index).wait_send()
                return carry

            lax.fori_loop(1, near_count, body, 0)

        def coarse_start(k):
            gather_wait(k)
            stacked = gathered[k].reshape(coarse_count * width, cases)
            part[k] = dot(partner_rows[...], stacked)
            pair_copy(k, part.at[k], part_in.at[k]).start()
            return dot(rows_ref[...], stacked)

        def precondition(k, solved, coarse_part, target):
            pair_copy(k, part.at[k], part_in.at[k]).wait_recv()
            combined = weigh(solved + dot_left_transposed(basis_ref[...], coarse_part + part_in[k]))
            target[...] = combined.reshape(faces, dofs, cases)
            return combined

        def invert_block(j):
            eliminate(inverse_ref, leaf_ref, panel_ref, entry_ref, j)

        def column_sum(value):
            return jnp.sum(value, axis=0, keepdims=True)

        def flat(ref):
            return ref[...].reshape(order, cases)

        near_start(0, loads_ref)
        far_face_start(0, loads_ref.at[core])
        far_start(0)
        pair_copy(2, rows_ref, partner_rows).start()
        own[1].wait()
        own[2].wait()
        scaling = 1.0 + masks_ref[...].astype(jnp.float32)
        faces_in_leaf = LEAF // dofs
        diagonal = lax.broadcasted_iota(jnp.int32, (LEAF, LEAF), 0) == lax.broadcasted_iota(
            jnp.int32, (LEAF, LEAF), 1
        )
        blocks = [slice(i * LEAF, (i + 1) * LEAF) for i in range(order // LEAF)]
        across = [
            jnp.concatenate([scaling[i * faces_in_leaf + f] for f in range(faces_in_leaf)], axis=1)
            for i in range(len(blocks))
        ]
        for i, rows in enumerate(blocks):
            down = jnp.sum(jnp.where(diagonal, across[i], 0.0), axis=1, keepdims=True)
            for j, columns in enumerate(blocks):
                operator_ref[rows, columns] = down * operator_ref[rows, columns] * across[j]
        inverse_ref[...] = operator_ref[...] + dot_left_transposed(basis_ref[...], basis_ref[...])
        half_of_lane = lax.broadcasted_iota(jnp.int32, (dofs, 2 * dofs), 1) // dofs
        corner = jnp.where(core == 0, operator_ref[:dofs, : 2 * dofs], operator_ref[dofs : 2 * dofs, : 2 * dofs])
        corner_out[...] = jnp.where(half_of_lane == core, corner, 0.0)
        slice_out[...] = jnp.where(half_of_lane[:width] == core, basis_ref[:, : 2 * dofs], 0.0)
        far_start(1)
        far_start(2)
        invert_block(0)
        near_wait(0)
        far_face_wait(0)
        r0 = flat(loads_ref) + flat(halo.at[0])
        weighted = weigh(r0)
        gather_start(0, weighted)
        invert_block(1)
        pair_copy(2, rows_ref, partner_rows).wait_recv()
        for n in range(3):
            far_wait(n)
        coarse_part = coarse_start(0)
        invert_block(2)
        u0 = precondition(0, dot(inverse_ref[...], weighted), coarse_part, unsummed.at[0])
        near_start(1, unsummed.at[0])
        far_face_start(1, unsummed.at[0, core])
        gamma_part = column_sum(r0 * u0)
        shared = unsummed[0, core]
        near_wait(1)
        near_z0 = u0 + near_incoming(1)
        near_t0 = dot(operator_ref[...], near_z0)
        far_out[0] = far_face_of(near_t0)
        far_face_start(2, far_out.at[0])
        corner_term = dot(corner_in[...], jnp.concatenate([shared, shared], axis=0))
        far_face_wait(1)
        arrived = on_far_face(halo[1, core])
        z0 = add_on_coarse_faces(near_z0, arrived)
        t0 = near_t0 + dot(operator_ref[:, : 2 * dofs], arrived)
        unsummed[1] = t0.reshape(faces, dofs, cases)
        near_start(2, unsummed.at[1])
        sum_start(0, 0, jnp.concatenate([gamma_part, column_sum(z0 * t0)], axis=0))
        near_wait(2)
        near_q0 = t0 + near_incoming(2)
        far_face_wait(2)
        q0 = add_on_coarse_faces(near_q0, on_far_face(halo[2, core] + corner_term))
        weighted = weigh(q0)
        gather_start(1, weighted)
        solved = weigh(dot(inverse_ref[...], weighted))
        far_out[1] = far_face_of(solved)
        far_face_start(3, far_out.at[1])
        sum_start(0, 1, sum_end(0, 0))
        coarse_part = coarse_start(1)
        own_out[...] = coarse_part
        far_start(3)
        far_coarse = dot(far_rows[...], gathered[1].reshape(coarse_count * width, cases))
        sum_start(0, 2, sum_end(0, 1))
        pair_copy(1, part.at[1], part_in.at[1]).wait_recv()
        u1 = solved + weigh(dot_left_transposed(basis_ref[...], coarse_part + part_in[1]))
        unsummed[2] = u1.reshape(faces, dofs, cases)
        near_start(3, unsummed.at[2])
        far_wait(3)
        far_face_wait(3)
        spread = 0.5 * dot_left_transposed(slice_in[...], far_coarse + own_in[...])
        far_w0 = add_on_coarse_faces(u1, on_far_face(halo[3, core] + spread[:dofs] + spread[dofs:]))
        near_wait(3)
        w0 = far_w0 + near_incoming(3)
        t1 = dot(operator_ref[...], w0)
        unsummed[3] = t1.reshape(faces, dofs, cases)
        near_start(4, unsummed.at[3])
        far_face_start(4, unsummed.at[3, core])
        first = sum_end(0, 2)
        gamma, energy = first[0:1], first[1:2]
        step = gamma / energy
        z1 = z0 - step * w0
        r1 = r0 - step * q0
        t1_next = t0 - step * t1
        sum_start(
            1,
            0,
            jnp.concatenate(
                [column_sum(r1 * (u0 - step * u1)), column_sum(z1 * t1_next), column_sum(z0 * t1_next), jnp.zeros_like(step)],
                axis=0,
            ),
        )
        sum_start(1, 1, sum_end(1, 0))
        sum_start(1, 2, sum_end(1, 1))
        near_wait(4)
        far_face_wait(4)
        mapped = q0 - step * (t1 + flat(halo.at[4]))
        second = sum_end(1, 2)
        gamma_next = second[0:1]
        ratio = gamma_next / gamma
        last = gamma_next / (second[1:2] + 2.0 * ratio * second[2:3] + ratio * ratio * energy)
        solution_ref[...] = (step * z0 + last * (z1 + ratio * z0)).reshape(faces, dofs, cases)
        residual_ref[...] = (r1 - last * (mapped + ratio * q0)).reshape(faces, dofs, cases)

        near_finish(0, loads_ref)
        far_face_finish(0, loads_ref.at[core])
        for k in range(1, 5):
            near_finish(k, unsummed.at[k - 1])
        far_face_finish(1, unsummed.at[0, core])
        far_face_finish(2, far_out.at[0])
        far_face_finish(3, far_out.at[1])
        far_face_finish(4, unsummed.at[3, core])
        for n in range(4):
            far_finish(n)
        pair_copy(2, rows_ref, partner_rows).wait_send()
        for k in range(2):
            gather_finish(k)
            pair_copy(k, part.at[k], part_in.at[k]).wait_send()
            for buffers, send, recv, mine, count, device_of in stages:
                spread_finish(buffers[k], send, recv, k, mine, count, device_of)

    return kernel


def on_device(sizes, face_loads, schur_blocks, coarse_basis, drop_masks, coarse_inverse):
    x_count, half_count, core_count, low_count, y_count, row_step = sizes
    coarse_count = x_count * half_count * core_count
    near_count, far_count = x_count * core_count, low_count * half_count
    faces, dofs, cases = face_loads.shape[2:]
    order = faces * dofs
    width = coarse_basis.shape[3]
    vector = jax.ShapeDtypeStruct((faces, dofs, cases), jnp.float32)
    dma = pltpu.SemaphoreType.DMA
    solved, residual = pl.pallas_call(
        make_iterate_kernel(sizes),
        out_shape=[vector, vector],
        in_specs=[
            pl.BlockSpec(memory_space=pl.ANY),
            pl.BlockSpec(memory_space=pl.ANY),
            pl.BlockSpec(memory_space=pl.ANY),
            pl.BlockSpec(memory_space=pltpu.VMEM),
            pl.BlockSpec(memory_space=pl.ANY),
        ],
        out_specs=[pl.BlockSpec(memory_space=pltpu.VMEM)] * 2,
        scratch_shapes=[
            pltpu.VMEM((faces, dofs, cases), jnp.float32),
            pltpu.VMEM((order, order), jnp.float32),
            pltpu.VMEM((width, order), jnp.float32),
            pltpu.VMEM((width, coarse_count * width), jnp.float32),
            pltpu.VMEM((order, order), jnp.float32),
            pltpu.VMEM((LEAF, LEAF), jnp.float32),
            pltpu.VMEM((GROUP, LEAF), jnp.float32),
            pltpu.VMEM((GROUP, GROUP, LEAF), jnp.float32),
            pltpu.VMEM((5, faces, dofs, cases), jnp.float32),
            pltpu.VMEM((4, faces, dofs, cases), jnp.float32),
            pltpu.VMEM((2, coarse_count, width, cases), jnp.float32),
            pltpu.VMEM((width, coarse_count * width), jnp.float32),
            pltpu.VMEM((2, width, cases), jnp.float32),
            pltpu.VMEM((2, width, cases), jnp.float32),
            pltpu.VMEM((2, dofs, cases), jnp.float32),
            pltpu.VMEM((dofs, 2 * dofs), jnp.float32),
            pltpu.VMEM((dofs, 2 * dofs), jnp.float32),
            pltpu.VMEM((width, 2 * dofs), jnp.float32),
            pltpu.VMEM((width, 2 * dofs), jnp.float32),
            pltpu.VMEM((width, coarse_count * width), jnp.float32),
            pltpu.VMEM((width, cases), jnp.float32),
            pltpu.VMEM((width, cases), jnp.float32),
            pltpu.VMEM((near_count, 2, cases), jnp.float32),
            pltpu.VMEM((y_count, 2, cases), jnp.float32),
            pltpu.VMEM((far_count, 2, cases), jnp.float32),
            pltpu.VMEM((near_count, 4, cases), jnp.float32),
            pltpu.VMEM((y_count, 4, cases), jnp.float32),
            pltpu.VMEM((far_count, 4, cases), jnp.float32),
            dma((4,)),
            dma((4,)),
            dma((4,)),
            dma((5, faces)),
            dma((5, faces)),
            dma((2, near_count)),
            dma((2, coarse_count)),
            dma((3,)),
            dma((3,)),
            dma((2, near_count)),
            dma((2, near_count)),
            dma((2, y_count)),
            dma((2, y_count)),
            dma((2, far_count)),
            dma((2, far_count)),
        ],
        compiler_params=pltpu.CompilerParams(
            collective_id=0, has_side_effects=True, vmem_limit_bytes=56 << 20
        ),
    )(face_loads[0, 0], schur_blocks[0, 0], coarse_basis[0, 0].T, drop_masks[0].transpose(1, 0, 2), coarse_inverse[0])
    return solved[None, None], residual[None, None]


def solution(mesh, sizes=(X_COUNT, HALF_COUNT, CORE_COUNT, LOW_COUNT, Y_COUNT, ROW)):
    def body(*arrays):
        return on_device(sizes, *arrays)

    return jax.shard_map(
        body,
        mesh=mesh,
        in_specs=(
            P("coarse", "sub", None, None, None),
            P("coarse", "sub", None, None),
            P("coarse", "sub", None, None),
            P("coarse", "sub", None, None),
            P("sub", "coarse", None),
        ),
        out_specs=(P("coarse", "sub", None, None, None), P("coarse", "sub", None, None, None)),
        check_vma=False,
    )
```

```python
import jax
import jax.numpy as jnp
from jax import lax
from jax.experimental import pallas as pl
from jax.experimental.pallas import tpu as pltpu
from jax.sharding import PartitionSpec as P

ROW = 8
X_COUNT, HALF_COUNT, CORE_COUNT = 4, 2, 2
LOW_COUNT, Y_COUNT = 8, 8
LEAF = 128
GROUP = 8
BEGIN_STEP, GATHER_STEP, COMBINE_STEP = 7, 7, 4

MESH = pl.DeviceIdType.MESH
highest = lax.Precision.HIGHEST


def dot(former, latter):
    return jnp.dot(former, latter, precision=highest, preferred_element_type=jnp.float32)


def dot_left_transposed(former, latter):
    return lax.dot_general(
        former, latter, (((0,), (0,)), ((), ())), precision=highest, preferred_element_type=jnp.float32
    )


def reciprocal(value):
    guess = pl.reciprocal(value, approx=True)
    return guess * (2.0 - value * guess)


def product(former, latter):
    out = []
    for row in former:
        line = []
        for j in range(len(latter[0])):
            total = row[0] * latter[0][j]
            for t in range(1, len(latter)):
                total = total + row[t] * latter[t][j]
            line.append(total)
        out.append(line)
    return out


def small_inverse(matrix):
    size = len(matrix)
    if size == 2:
        a, b, c = matrix[0][0], matrix[0][1], matrix[1][1]
        det = reciprocal(a * c - b * b)
        return [[c * det, -b * det], [-b * det, a * det]]
    first, carried, second = halves(matrix)
    half = size // 2
    side = product(carried, second)
    out = [[None] * size for _ in range(size)]
    for i in range(half):
        for j in range(i, half):
            total = first[i][j]
            for t in range(half):
                total = total + side[i][t] * carried[j][t]
            out[i][j] = out[j][i] = total
        for j in range(half):
            out[i][half + j] = out[half + j][i] = -side[i][j]
            out[half + i][half + j] = second[i][j]
    return out


def halves(matrix):
    half = len(matrix) // 2
    corner = [row[half:] for row in matrix[:half]]
    first = small_inverse([row[:half] for row in matrix[:half]])
    carried = product(first, corner)
    rest = [[None] * half for _ in range(half)]
    for i in range(half):
        for j in range(i, half):
            total = matrix[half + i][half + j]
            for t in range(half):
                total = total - corner[t][i] * carried[t][j]
            rest[i][j] = rest[j][i] = total
    return first, carried, small_inverse(rest)


def small_solve(matrix, right):
    half = len(matrix) // 2
    first, carried, second = halves(matrix)
    lower = []
    for i in range(half):
        total = right[half + i]
        for t in range(half):
            total = total - carried[t][i] * right[t]
        lower.append(total)
    upper = [row[0] for row in product(first, [[value] for value in right[:half]])]
    below = [row[0] for row in product(second, [[value] for value in lower])]
    above = []
    for i in range(half):
        total = upper[i]
        for t in range(half):
            total = total - carried[i][t] * below[t]
        above.append(total)
    return above + below


def invert_leaf(leaf_ref, panel_ref, entry_ref, visits):
    shape = (GROUP, LEAF)
    lane = lax.broadcasted_iota(jnp.int32, shape, 1)
    sublane = lax.broadcasted_iota(jnp.int32, shape, 0)
    wide_lane = lax.broadcasted_iota(jnp.int32, (LEAF, LEAF), 1)
    last = LEAF - GROUP

    def solve(panel):
        for s in range(GROUP):
            entry_ref[s] = jnp.broadcast_to(panel[:, s : s + 1], shape)
        pivots = [[None] * GROUP for _ in range(GROUP)]
        for r in range(GROUP):
            for s in range(r, GROUP):
                pivots[r][s] = pivots[s][r] = jnp.broadcast_to(entry_ref[s, r : r + 1, :], shape)
        turned = jnp.where(lane >= last, 0.0, pltpu.roll(panel, last, 1))
        panel_ref[...] = jnp.where(lane == last + sublane, 1.0, turned)
        unit = [jnp.broadcast_to(panel_ref[t : t + 1, :], shape) for t in range(GROUP)]
        return small_solve(pivots, unit)

    def tile_of(solved):
        tile = solved[0]
        for s in range(1, GROUP):
            tile = jnp.where(sublane == s, solved[s], tile)
        return tile

    def update(tile):
        old = leaf_ref[...]
        turned = jnp.where(wide_lane >= last, 0.0, pltpu.roll(old, last, 1))
        return turned - dot(old[:, :GROUP], tile)

    def step(g, solved):
        tile = tile_of(solved)
        old = leaf_ref[pl.ds(pl.multiple_of((g + 1) * GROUP, GROUP), GROUP), :]
        panel = jnp.where(lane >= last, 0.0, pltpu.roll(old, last, 1))
        for s in range(GROUP):
            panel = panel - jnp.broadcast_to(old[:, s : s + 1], shape) * solved[s]
        following = solve(panel)
        new = update(tile)
        for i in range(LEAF // GROUP):
            rows = slice(i * GROUP, (i + 1) * GROUP)
            leaf_ref[rows, :] = jnp.where(g == i, tile, jnp.where(g + 1 == i, panel, new[rows]))
        return following

    solved = solve(leaf_ref[:GROUP, :])
    done = 0
    for until, visit in list(visits) + [(LEAF // GROUP - 1, None)]:
        solved = lax.fori_loop(done, until, step, solved)
        done = until
        if visit is not None:
            visit()
    new = update(tile_of(solved))
    leaf_ref[:last, :] = new[:last]
    leaf_ref[last:, :] = tile_of(solved)


def eliminate(matrix_ref, leaf_ref, panel_ref, entry_ref, j, visits=()):
    blocks = matrix_ref.shape[0] // LEAF
    here = slice(j * LEAF, (j + 1) * LEAF)
    leaf_ref[...] = matrix_ref[here, here]
    invert_leaf(leaf_ref, panel_ref, entry_ref, visits)
    inverse = leaf_ref[...]
    matrix_ref[here, here] = inverse
    others = [slice(i * LEAF, (i + 1) * LEAF) for i in range(blocks) if i != j]
    for columns in others:
        matrix_ref[here, columns] = dot(inverse, matrix_ref[here, columns])
    for rows in others:
        column = matrix_ref[rows, here]
        for columns in others:
            matrix_ref[rows, columns] = matrix_ref[rows, columns] - dot(column, matrix_ref[here, columns])
        matrix_ref[rows, here] = -dot(column, inverse)


def make_iterate_kernel(sizes):
    x_count, half_count, core_count, low_count, y_count, row_step = sizes
    coarse_count = x_count * half_count * core_count
    sub_count = low_count * y_count
    near_count = x_count * core_count
    far_count = low_count * half_count

    def kernel(
        loads_hbm, schur_hbm, basis_hbm, masks_hbm, rows_hbm, solution_ref, residual_ref,
        loads_ref, schur_ref, basis_ref, masks_ref, rows_ref, own_sem, start_ref, coarse_ref, operator_ref, inverse_ref, leaf_ref, panel_ref, entry_ref,
        halo, unsummed, gathered, rows_own, rows_cross, partner_rows, part, part_in,
        far_out, corner_out, corner_in, slice_out, slice_in, far_rows, own_out, own_in,
        sums_1a, sums_1b, sums_1c, sums_2a, sums_2b, sums_2c,
        far_send, far_recv,
        halo_send, halo_recv, near_send, near_recv, pair_send, pair_recv,
        a_send, a_recv, b_send, b_recv, c_send, c_recv,
    ):
        own = []
        for n, (source, target) in enumerate(
            [
                (schur_hbm, schur_ref),
                (basis_hbm, basis_ref),
                (masks_hbm, masks_ref),
                (loads_hbm, loads_ref),
                (rows_hbm, rows_ref),
            ]
        ):
            own.append(pltpu.make_async_copy(source, target, own_sem.at[n]))
            own[n].start()
        faces, dofs, cases = loads_ref.shape
        order = faces * dofs
        width = basis_ref.shape[0]
        coarse = lax.axis_index("coarse")
        sub = lax.axis_index("sub")
        core = coarse % core_count
        half = (coarse // core_count) % half_count
        x = coarse // (core_count * half_count)
        y = sub % y_count
        low = sub // y_count
        near = x * core_count + core
        far = low * half_count + half

        def near_device(index):
            return ((index // core_count * half_count + half) * core_count + index % core_count, sub)

        def y_device(index):
            return (coarse, low * y_count + index)

        def far_device(index):
            return ((x * half_count + index % half_count) * core_count + core, index // half_count * y_count + y)

        partner = ((x * half_count + (half_count - 1 - half)) * core_count + core, sub)
        present = [
            coarse > 0,
            coarse < coarse_count - 1,
            sub > 0,
            sub < sub_count - 1,
            sub >= row_step,
            sub < sub_count - row_step,
        ]
        neighbour = [
            (coarse - 1, sub),
            (coarse + 1, sub),
            (coarse, sub - 1),
            (coarse, sub + 1),
            (coarse, sub - row_step),
            (coarse, sub + row_step),
        ]

        barrier = pltpu.get_barrier_semaphore()

        def greet(device):
            pl.semaphore_signal(barrier, inc=1, device_id=device, device_id_type=MESH)

        expected = near_count + y_count + far_count - 3
        for face in range(faces):
            expected = expected + present[face].astype(jnp.int32)

            @pl.when(present[face])
            def _():
                greet(neighbour[face])

        lax.fori_loop(1, far_count, lambda j, c: (greet(far_device((far + j) % far_count)), c)[1], 0)
        lax.fori_loop(1, y_count, lambda j, c: (greet(y_device((y + j) % y_count)), c)[1], 0)
        lax.fori_loop(1, near_count, lambda j, c: (greet(near_device((near + j) % near_count)), c)[1], 0)

        weights = [jnp.where(present[face], 0.5, 1.0) for face in range(faces)]
        for face in range(faces):

            @pl.when(jnp.logical_not(present[face]))
            def _():
                for k in range(halo.shape[0]):
                    halo[k, face] = jnp.zeros((dofs, cases), jnp.float32)


        far_present = jnp.logical_or(
            jnp.logical_and(core == 0, present[0]), jnp.logical_and(core == 1, present[1])
        )
        far_device_id = (coarse - 1 + 2 * core, sub)

        @pl.when(jnp.logical_not(far_present))
        def _():
            for buffer in (corner_in, slice_in, far_rows, own_in):
                buffer[...] = jnp.zeros_like(buffer)

        def face_copy(k, source, face, device):
            return pltpu.make_async_remote_copy(
                src_ref=source,
                dst_ref=halo.at[k, face ^ 1],
                send_sem=halo_send.at[k, face],
                recv_sem=halo_recv.at[k, face ^ 1],
                device_id=device,
                device_id_type=MESH,
            )

        def near_faces(action):
            for face in range(faces):
                here = present[face]
                if face < 2:
                    here = jnp.logical_and(here, core != face)

                @pl.when(here)
                def _():
                    action(face)

        def near_start(k, source):
            near_faces(lambda face: face_copy(k, source.at[face], face, neighbour[face]).start())

        def near_wait(k):
            near_faces(lambda face: face_copy(k, halo.at[k, face], face ^ 1, neighbour[face]).wait_recv())

        def near_finish(k, source):
            near_faces(lambda face: face_copy(k, source.at[face], face, neighbour[face]).wait_send())

        def far_face_copy(k, source):
            return pltpu.make_async_remote_copy(
                src_ref=source,
                dst_ref=halo.at[k, 1 - core],
                send_sem=halo_send.at[k, core],
                recv_sem=halo_recv.at[k, 1 - core],
                device_id=far_device_id,
                device_id_type=MESH,
            )

        def far_face_start(k, source):
            @pl.when(far_present)
            def _():
                far_face_copy(k, source).start()

        def far_face_wait(k):
            @pl.when(far_present)
            def _():
                pltpu.make_async_remote_copy(
                    src_ref=halo.at[k, core],
                    dst_ref=halo.at[k, core],
                    send_sem=halo_send.at[k, 1 - core],
                    recv_sem=halo_recv.at[k, core],
                    device_id=far_device_id,
                    device_id_type=MESH,
                ).wait_recv()

        def far_face_finish(k, source):
            @pl.when(far_present)
            def _():
                far_face_copy(k, source).wait_send()

        def far_copy(n, source, target):
            return pltpu.make_async_remote_copy(
                src_ref=source,
                dst_ref=target,
                send_sem=far_send.at[n],
                recv_sem=far_recv.at[n],
                device_id=far_device_id,
                device_id_type=MESH,
            )

        far_pairs = [(rows_cross, far_rows), (corner_out, corner_in), (slice_out, slice_in), (own_out, own_in)]

        def far_start(n):
            @pl.when(far_present)
            def _():
                far_copy(n, *far_pairs[n]).start()

        def far_wait(n):
            @pl.when(far_present)
            def _():
                far_copy(n, *far_pairs[n]).wait_recv()

        def far_finish(n):
            @pl.when(far_present)
            def _():
                far_copy(n, *far_pairs[n]).wait_send()

        def near_incoming(k):
            sibling = halo[k, 1 - core]
            pieces = [jnp.where(core == 1, sibling, 0.0), jnp.where(core == 0, sibling, 0.0)]
            return jnp.concatenate(pieces + [halo[k, face] for face in range(2, faces)], axis=0)

        def on_far_face(value):
            return jnp.concatenate([jnp.where(core == 0, value, 0.0), jnp.where(core == 1, value, 0.0)], axis=0)

        def far_face_of(value):
            return jnp.where(core == 0, value[:dofs], value[dofs : 2 * dofs])

        def add_on_coarse_faces(value, extra):
            return jnp.concatenate([value[: 2 * dofs] + extra, value[2 * dofs :]], axis=0)

        def pair_copy(k, source, target):
            return pltpu.make_async_remote_copy(
                src_ref=source,
                dst_ref=target,
                send_sem=pair_send.at[k],
                recv_sem=pair_recv.at[k],
                device_id=partner,
                device_id_type=MESH,
            )

        def spread_copy(buffer, send, recv, k, mine, device, slot, index):
            return pltpu.make_async_remote_copy(
                src_ref=buffer.at[mine],
                dst_ref=buffer.at[slot],
                send_sem=send.at[k, index],
                recv_sem=recv.at[k, slot],
                device_id=device,
                device_id_type=MESH,
            )

        def spread_start(buffer, send, recv, k, mine, count, device_of):
            def body(j, carry):
                index = (mine + j) % count
                spread_copy(buffer, send, recv, k, mine, device_of(index), mine, index).start()
                return carry

            lax.fori_loop(1, count, body, 0)

        def spread_wait(buffer, send, recv, k, mine, count, device_of):
            def body(j, carry):
                index = (mine + j) % count
                spread_copy(buffer, send, recv, k, mine, device_of(index), index, index).wait_recv()
                return carry

            lax.fori_loop(1, count, body, 0)

        def spread_finish(buffer, send, recv, k, mine, count, device_of):
            def body(j, carry):
                index = (mine + j) % count
                spread_copy(buffer, send, recv, k, mine, device_of(index), mine, index).wait_send()
                return carry

            lax.fori_loop(1, count, body, 0)

        stages = [
            ((sums_1a, sums_2a), a_send, a_recv, near, near_count, near_device),
            ((sums_1b, sums_2b), b_send, b_recv, y, y_count, y_device),
            ((sums_1c, sums_2c), c_send, c_recv, far, far_count, far_device),
        ]

        def sum_start(k, stage, value):
            buffers, send, recv, mine, count, device_of = stages[stage]
            buffer = buffers[k]
            buffer[mine] = value
            spread_start(buffer, send, recv, k, mine, count, device_of)

        def sum_end(k, stage):
            buffers, send, recv, mine, count, device_of = stages[stage]
            buffer = buffers[k]
            spread_wait(buffer, send, recv, k, mine, count, device_of)
            total = buffer[0]
            for index in range(1, count):
                total = total + buffer[index]
            return total

        def weigh(vector):
            pieces = [vector[face * dofs : (face + 1) * dofs] * weights[face] for face in range(faces)]
            return jnp.concatenate(pieces, axis=0)

        def gather_start(k, weighted):
            gathered[k, near] = dot(basis_ref[...], weighted)
            spread_start(gathered.at[k], near_send, near_recv, k, near, near_count, near_device)

        def gather_wait(k):
            spread_wait(gathered.at[k], near_send, near_recv, k, near, near_count, near_device)

        def gather_finish(k):
            spread_finish(gathered.at[k], near_send, near_recv, k, near, near_count, near_device)

        def coarse_start(k):
            gather_wait(k)
            stacked = gathered[k].reshape(near_count * width, cases)
            part[k] = dot(partner_rows[...], stacked)
            pair_copy(k, part.at[k], part_in.at[k]).start()
            return dot(rows_own[...], stacked)

        def precondition(k, solved, coarse_part, target):
            pair_copy(k, part.at[k], part_in.at[k]).wait_recv()
            combined = weigh(solved + dot_left_transposed(basis_ref[...], coarse_part + part_in[k]))
            target[...] = combined.reshape(faces, dofs, cases)
            return combined

        def invert_block(j, *visits):
            eliminate(inverse_ref, leaf_ref, panel_ref, entry_ref, j, visits)

        def column_sum(value):
            return jnp.sum(value, axis=0, keepdims=True)

        def flat(ref):
            return ref[...].reshape(order, cases)

        for copy in own:
            copy.wait()
        scaling = 1.0 + masks_ref[...].astype(jnp.float32)
        faces_in_leaf = LEAF // dofs
        diagonal = lax.broadcasted_iota(jnp.int32, (LEAF, LEAF), 0) == lax.broadcasted_iota(
            jnp.int32, (LEAF, LEAF), 1
        )
        blocks = [slice(i * LEAF, (i + 1) * LEAF) for i in range(order // LEAF)]
        across = [
            jnp.concatenate([scaling[i * faces_in_leaf + f] for f in range(faces_in_leaf)], axis=1)
            for i in range(len(blocks))
        ]
        for i, rows in enumerate(blocks):
            down = jnp.sum(jnp.where(diagonal, across[i], 0.0), axis=1, keepdims=True)
            for j, columns in enumerate(blocks):
                operator_ref[rows, columns] = down * schur_ref[rows, columns] * across[j]
        inverse_ref[...] = operator_ref[...] + dot_left_transposed(basis_ref[...], basis_ref[...])

        piece = core_count * width

        def columns_of(which):
            pieces = []
            for index in range(x_count):
                at = index * half_count * piece
                pieces.append(
                    jnp.where(which == 0, rows_ref[:, at : at + piece], rows_ref[:, at + piece : at + 2 * piece])
                )
            return jnp.concatenate(pieces, axis=1)

        rows_cross[...] = columns_of(1 - half)
        rows_own[...] = columns_of(half)
        corner = jnp.where(core == 0, operator_ref[:dofs, :dofs], operator_ref[dofs : 2 * dofs, dofs : 2 * dofs])
        corner_out[...] = jnp.concatenate([corner[: dofs // 2], corner[dofs // 2 :]], axis=1)
        basis_slice = jnp.where(core == 0, basis_ref[:, :dofs], basis_ref[:, dofs : 2 * dofs])
        slice_out[...] = jnp.concatenate([basis_slice[: width // 2], basis_slice[width // 2 :]], axis=1)

        def begin():
            pl.semaphore_wait(barrier, expected)
            far_face_start(0, loads_ref.at[core])
            near_start(0, loads_ref)

        def send_rows():
            pair_copy(2, rows_cross, partner_rows).start()

        def gather_loads():
            near_wait(0)
            far_face_wait(0)
            r0 = flat(loads_ref) + flat(halo.at[0])
            start_ref[...] = r0
            gather_start(0, weigh(r0))
            for n in range(3):
                far_start(n)

        def combine_loads():
            pair_copy(2, rows_cross, partner_rows).wait_recv()
            coarse_ref[...] = coarse_start(0)

        invert_block(0, (BEGIN_STEP, begin), (LEAF // GROUP - 1, send_rows))
        invert_block(1, (GATHER_STEP, gather_loads))
        invert_block(2, (COMBINE_STEP, combine_loads))
        r0 = start_ref[...]
        u0 = precondition(0, dot(inverse_ref[...], weigh(r0)), coarse_ref[...], unsummed.at[0])
        near_start(1, unsummed.at[0])
        far_face_start(1, unsummed.at[0, core])
        gamma_part = column_sum(r0 * u0)
        shared = unsummed[0, core]
        near_wait(1)
        near_z0 = u0 + near_incoming(1)
        near_t0 = dot(operator_ref[...], near_z0)
        far_out[0] = far_face_of(near_t0)
        far_face_start(2, far_out.at[0])
        for n in range(3):
            far_wait(n)
        corner = jnp.concatenate([corner_in[:, :dofs], corner_in[:, dofs:]], axis=0)
        corner_term = dot(corner, shared)
        far_face_wait(1)
        arrived = on_far_face(halo[1, core])
        z0 = add_on_coarse_faces(near_z0, arrived)
        t0 = near_t0 + dot(operator_ref[:, : 2 * dofs], arrived)
        unsummed[1] = t0.reshape(faces, dofs, cases)
        near_start(2, unsummed.at[1])
        sum_start(0, 0, jnp.concatenate([gamma_part, column_sum(z0 * t0)], axis=0))
        near_wait(2)
        near_q0 = t0 + near_incoming(2)
        far_face_wait(2)
        q0 = add_on_coarse_faces(near_q0, on_far_face(halo[2, core] + corner_term))
        weighted = weigh(q0)
        gather_start(1, weighted)
        solved = weigh(dot(inverse_ref[...], weighted))
        far_out[1] = far_face_of(solved)
        far_face_start(3, far_out.at[1])
        sum_start(0, 1, sum_end(0, 0))
        coarse_part = coarse_start(1)
        own_out[...] = coarse_part
        far_start(3)
        far_coarse = dot(far_rows[...], gathered[1].reshape(near_count * width, cases))
        sum_start(0, 2, sum_end(0, 1))
        pair_copy(1, part.at[1], part_in.at[1]).wait_recv()
        u1 = solved + weigh(dot_left_transposed(basis_ref[...], coarse_part + part_in[1]))
        unsummed[2] = u1.reshape(faces, dofs, cases)
        near_start(3, unsummed.at[2])
        far_wait(3)
        far_face_wait(3)
        basis_slice = jnp.concatenate([slice_in[:, :dofs], slice_in[:, dofs:]], axis=0)
        spread = 0.5 * dot_left_transposed(basis_slice, far_coarse + own_in[...])
        far_w0 = add_on_coarse_faces(u1, on_far_face(halo[3, core] + spread))
        near_wait(3)
        w0 = far_w0 + near_incoming(3)
        t1 = dot(operator_ref[...], w0)
        unsummed[3] = t1.reshape(faces, dofs, cases)
        near_start(4, unsummed.at[3])
        far_face_start(4, unsummed.at[3, core])
        first = sum_end(0, 2)
        gamma, energy = first[0:1], first[1:2]
        step = gamma / energy
        z1 = z0 - step * w0
        r1 = r0 - step * q0
        t1_next = t0 - step * t1
        sum_start(
            1,
            0,
            jnp.concatenate(
                [column_sum(r1 * (u0 - step * u1)), column_sum(z1 * t1_next), column_sum(z0 * t1_next), jnp.zeros_like(step)],
                axis=0,
            ),
        )
        sum_start(1, 1, sum_end(1, 0))
        sum_start(1, 2, sum_end(1, 1))
        near_wait(4)
        far_face_wait(4)
        mapped = q0 - step * (t1 + flat(halo.at[4]))
        second = sum_end(1, 2)
        gamma_next = second[0:1]
        ratio = gamma_next / gamma
        last = gamma_next / (second[1:2] + 2.0 * ratio * second[2:3] + ratio * ratio * energy)
        solution_ref[...] = (step * z0 + last * (z1 + ratio * z0)).reshape(faces, dofs, cases)
        residual_ref[...] = (r1 - last * (mapped + ratio * q0)).reshape(faces, dofs, cases)

        near_finish(0, loads_ref)
        far_face_finish(0, loads_ref.at[core])
        for k in range(1, 5):
            near_finish(k, unsummed.at[k - 1])
        far_face_finish(1, unsummed.at[0, core])
        far_face_finish(2, far_out.at[0])
        far_face_finish(3, far_out.at[1])
        far_face_finish(4, unsummed.at[3, core])
        for n in range(4):
            far_finish(n)
        pair_copy(2, rows_cross, partner_rows).wait_send()
        for k in range(2):
            gather_finish(k)
            pair_copy(k, part.at[k], part_in.at[k]).wait_send()
            for buffers, send, recv, mine, count, device_of in stages:
                spread_finish(buffers[k], send, recv, k, mine, count, device_of)

    return kernel


def on_device(sizes, face_loads, schur_blocks, coarse_basis, drop_masks, coarse_inverse):
    x_count, half_count, core_count, low_count, y_count, row_step = sizes
    coarse_count = x_count * half_count * core_count
    near_count, far_count = x_count * core_count, low_count * half_count
    faces, dofs, cases = face_loads.shape[2:]
    order = faces * dofs
    width = coarse_basis.shape[3]
    vector = jax.ShapeDtypeStruct((faces, dofs, cases), jnp.float32)
    dma = pltpu.SemaphoreType.DMA
    solved, residual = pl.pallas_call(
        make_iterate_kernel(sizes),
        out_shape=[vector, vector],
        in_specs=[pl.BlockSpec(memory_space=pl.ANY)] * 5,
        out_specs=[pl.BlockSpec(memory_space=pltpu.VMEM)] * 2,
        scratch_shapes=[
            pltpu.VMEM((faces, dofs, cases), jnp.float32),
            pltpu.VMEM((order, order), jnp.float32),
            pltpu.VMEM((width, order), jnp.float32),
            pltpu.VMEM((faces, 1, dofs), jnp.int32),
            pltpu.VMEM((width, coarse_count * width), jnp.float32),
            dma((5,)),
            pltpu.VMEM((order, cases), jnp.float32),
            pltpu.VMEM((width, cases), jnp.float32),
            pltpu.VMEM((order, order), jnp.float32),
            pltpu.VMEM((order, order), jnp.float32),
            pltpu.VMEM((LEAF, LEAF), jnp.float32),
            pltpu.VMEM((GROUP, LEAF), jnp.float32),
            pltpu.VMEM((GROUP, GROUP, LEAF), jnp.float32),
            pltpu.VMEM((5, faces, dofs, cases), jnp.float32),
            pltpu.VMEM((4, faces, dofs, cases), jnp.float32),
            pltpu.VMEM((2, near_count, width, cases), jnp.float32),
            pltpu.VMEM((width, near_count * width), jnp.float32),
            pltpu.VMEM((width, near_count * width), jnp.float32),
            pltpu.VMEM((width, near_count * width), jnp.float32),
            pltpu.VMEM((2, width, cases), jnp.float32),
            pltpu.VMEM((2, width, cases), jnp.float32),
            pltpu.VMEM((2, dofs, cases), jnp.float32),
            pltpu.VMEM((dofs // 2, 2 * dofs), jnp.float32),
            pltpu.VMEM((dofs // 2, 2 * dofs), jnp.float32),
            pltpu.VMEM((width // 2, 2 * dofs), jnp.float32),
            pltpu.VMEM((width // 2, 2 * dofs), jnp.float32),
            pltpu.VMEM((width, near_count * width), jnp.float32),
            pltpu.VMEM((width, cases), jnp.float32),
            pltpu.VMEM((width, cases), jnp.float32),
            pltpu.VMEM((near_count, 2, cases), jnp.float32),
            pltpu.VMEM((y_count, 2, cases), jnp.float32),
            pltpu.VMEM((far_count, 2, cases), jnp.float32),
            pltpu.VMEM((near_count, 4, cases), jnp.float32),
            pltpu.VMEM((y_count, 4, cases), jnp.float32),
            pltpu.VMEM((far_count, 4, cases), jnp.float32),
            dma((4,)),
            dma((4,)),
            dma((5, faces)),
            dma((5, faces)),
            dma((2, near_count)),
            dma((2, near_count)),
            dma((3,)),
            dma((3,)),
            dma((2, near_count)),
            dma((2, near_count)),
            dma((2, y_count)),
            dma((2, y_count)),
            dma((2, far_count)),
            dma((2, far_count)),
        ],
        compiler_params=pltpu.CompilerParams(
            collective_id=0, has_side_effects=True, vmem_limit_bytes=56 << 20
        ),
    )(face_loads[0, 0], schur_blocks[0, 0], coarse_basis[0, 0].T, drop_masks[0].transpose(1, 0, 2), coarse_inverse[0])
    return solved[None, None], residual[None, None]


def solution(mesh, sizes=(X_COUNT, HALF_COUNT, CORE_COUNT, LOW_COUNT, Y_COUNT, ROW)):
    def body(*arrays):
        return on_device(sizes, *arrays)

    return jax.shard_map(
        body,
        mesh=mesh,
        in_specs=(
            P("coarse", "sub", None, None, None),
            P("coarse", "sub", None, None),
            P("coarse", "sub", None, None),
            P("coarse", "sub", None, None),
            P("sub", "coarse", None),
        ),
        out_specs=(P("coarse", "sub", None, None, None), P("coarse", "sub", None, None, None)),
        check_vma=False,
    )
```
